32 devices in a mesh: group: 2 (over y), inner: 4 (over z), outer: 2 (over x), cuts: 2 (over core).
Axes of the slice: x: 2, y: 2, z: 4, core: 2. Of those that a mesh axis runs over, the one named last changes fastest.
Arguments:
- volume: bfloat16 [96, 128, 256], P(('group', 'inner', 'outer'), None, 'cuts'), parts along dimension 0, may hold values from -6 to 6
- projector: bfloat16 [256, 4, 128, 128], P(('inner', 'outer')), may hold values from 0.19921875 to 1
- slot_ray: int32 [256], P(('inner', 'outer')), may hold values from 0 to 63, as said below
- slot_pixel: int32 [256, 4], P(('inner', 'outer')), may hold values from 0 to 5, as said below
- sinogram: bfloat16 [128, 128, 256], P(('group', 'inner', 'outer'), None, 'cuts'), parts along dimension 0, may hold values from -240 to 240
- weight_index: int32 [128, 128], P(('group', 'inner', 'outer')), parts along dimension 0, may hold values from 0 to 15
- weight_table: bfloat16 [16], replicated, may hold values from 0.099609375 to 1
Outputs:
- updated: float32 [96, 128, 256], P(('group', 'inner', 'outer'), None, 'cuts'), parts along dimension 0
The draws below stay inside these ranges and needn't reach their ends.
There are 2 independent parts, one for each index of `group`. The reference program is written for one: setup_inputs(seed, part) draws one part's arguments, and reference() takes and returns one part's arrays. A program takes and returns all parts, laid end to end along the dimension named above; an argument that names none is the same for every part. Nothing has to cross between parts.
Inputs may be any that keep to these rules, and one draw needn't show every extreme that they name: `slot_ray`: each patch lists 32 ray tiles, possibly some more than once. At most 16 of one patch's slots name ray tiles of one band k * 16 to (k + 1) * 16 - 1, and in every draw some band receives exactly 16 slots from every patch. `slot_pixel`: the 4 entries of a slot are different pixel tiles of its own patch; every pixel tile of a patch is named by some slot of that patch.
All inputs are finite; a program needn't handle non-finite values.
Results may differ from the reference program's by a relative error of at most 0.0003.
Values may be sent and summed in bfloat16 or wider, within the bound.
No kernel may reach another device: no remote copies, remote signals or barrier semaphores. Data moves between devices by JAX's collectives and lax.ppermute only.
A program may use at most 64 MiB of HBM per device.

```python
import math
import jax
import jax.numpy as jnp
from jax import lax

TILE = 128
PATCH_TILES = 6
SLOTS_DEV = 32
TILES_SLOT = 4
CLASSES = 16
PIX_TILES = 48
SLOTS = 256
RAY_TILES = 64
BAND = 16
CAPACITY = 16
SLICES = 256
N_INNER = 4
N_OUTER = 2


def draw_slot_ray(key, part):
    base_key = jax.random.fold_in(key, 101)
    key_hot, key_score, key_offset, key_order = jax.random.split(base_key, 4)
    patches = N_INNER * N_OUTER
    cell_count = N_INNER * CAPACITY
    hot_inner = jax.random.randint(key_hot, (), 0, N_INNER)
    cell_index = jnp.arange(cell_count, dtype=jnp.int32)
    dest_inner = cell_index // CAPACITY
    scores = jax.random.randint(key_score, (patches, cell_count), 0, 2 ** 16) * cell_count + cell_index[None, :]
    scores = scores + jnp.where(dest_inner == hot_inner, 2 ** 29, 0).astype(jnp.int32)[None, :]
    chosen = lax.top_k(scores, SLOTS_DEV)[1]
    order_scores = jax.random.randint(key_order, (patches, SLOTS_DEV), 0, 2 ** 16) * SLOTS_DEV + jnp.arange(SLOTS_DEV, dtype=jnp.int32)[None, :]
    shuffle = lax.top_k(order_scores, SLOTS_DEV)[1]
    chosen = jnp.take_along_axis(chosen, shuffle, axis=1)
    offsets = jax.random.randint(key_offset, (patches, SLOTS_DEV), 0, BAND)
    ray_rows = chosen // CAPACITY * BAND + offsets
    return ray_rows.reshape(-1).astype(jnp.int32)


def draw_slot_pixel(key, part):
    base_key = jax.random.fold_in(key, 202)
    slot_total = N_INNER * N_OUTER * SLOTS_DEV
    scores = jax.random.randint(base_key, (slot_total, PATCH_TILES), 0, 2 ** 16) * PATCH_TILES + jnp.arange(PATCH_TILES, dtype=jnp.int32)[None, :]
    shuffle = lax.top_k(scores, PATCH_TILES)[1]
    leading = shuffle[:, :1]
    wanted = (jnp.arange(slot_total, dtype=jnp.int32) % SLOTS_DEV % PATCH_TILES)[:, None]
    rolled = (shuffle - leading + wanted) % PATCH_TILES
    return rolled[:, :TILES_SLOT].astype(jnp.int32)


def set_ends(array, rng, low, top_value):
    longest = array.shape.index(max(array.shape))
    spots = []
    for shift in (0, 1):
        where = [jax.random.randint(jax.random.fold_in(rng, axis), (), 0, length) for axis, length in enumerate(array.shape)]
        where[longest] = (where[longest] + shift) % array.shape[longest]
        spots.append(tuple(where))
    return array.at[spots[0]].set(low).at[spots[1]].set(top_value)


def shard_levels(stream_key, extent, cuts, smallest, top_value):
    factor_of, own = 1.0, jax.random.fold_in(stream_key, 6)
    for dim, parts in cuts:
        heights = jnp.exp(jax.random.uniform(jax.random.fold_in(own, dim), (parts,), jnp.float32, smallest / len(cuts), top_value / len(cuts)))
        factor_of = factor_of * jnp.repeat(heights, extent[dim] // parts).reshape([-1 if axis == dim else 1 for axis in range(len(extent))])
    return factor_of


def centred(stream_key, extent, deviation, reach, cuts=(), kind=jnp.bfloat16):
    entries = deviation * jax.random.normal(stream_key, extent, jnp.float32)
    if cuts:
        entries = entries * shard_levels(stream_key, extent, cuts, -0.22, 0.18)
    return jnp.clip(entries, -reach, reach).astype(kind)


def setup_inputs(seed: int = 0, part: int = 0) -> dict:
    arg_keys = jax.random.split(jax.random.key(seed), 8)
    part_splits = jax.random.split(jax.random.fold_in(arg_keys[7], part), 8)
    volume = centred(part_splits[0], (PIX_TILES, TILE, SLICES), 1.0, 6.0, ((0, 8), (2, 2)))
    projector = jnp.clip(0.19921875 + 0.80078125 * jax.random.uniform(arg_keys[1], (SLOTS, TILES_SLOT, TILE, TILE), jnp.float32) ** shard_levels(arg_keys[1], (SLOTS, TILES_SLOT, TILE, TILE), ((0, 8),), -0.2, 0.2), 0.19921875, 1.0).astype(jnp.bfloat16)
    slot_ray = draw_slot_ray(jax.random.fold_in(arg_keys[7], 71), part)
    slot_pixel = draw_slot_pixel(jax.random.fold_in(arg_keys[7], 71), part)
    sinogram = centred(part_splits[4], (RAY_TILES, TILE, SLICES), 40.0, 240.0, ((0, 8), (2, 2)))
    weight_index = set_ends(jax.random.randint(part_splits[5], (RAY_TILES, TILE), 0, CLASSES), jax.random.fold_in(part_splits[5], 1), 0, CLASSES - 1).astype(jnp.int32)
    weight_table = jnp.clip(jnp.exp(jax.random.uniform(arg_keys[6], (CLASSES,), jnp.float32, math.log(0.099609375), math.log(1.0))), 0.099609375, 1.0).astype(jnp.bfloat16)
    return {"volume": volume, "projector": projector, "slot_ray": slot_ray, "slot_pixel": slot_pixel, "sinogram": sinogram, "weight_index": weight_index, "weight_table": weight_table}


def reference(volume, projector, slot_ray, slot_pixel, sinogram, weight_index, weight_table):
    patches = N_INNER * N_OUTER
    slot_count = projector.shape[0] // patches
    per_slot = projector.shape[1]
    tile_size = projector.shape[2]
    patch_tiles = volume.shape[0] // patches
    slice_count = volume.shape[2]
    ray_count = sinogram.shape[0]
    patch_base = (jnp.arange(projector.shape[0], dtype=jnp.int32) // slot_count) * patch_tiles
    pixel_index = (patch_base[:, None] + slot_pixel).astype(jnp.int32)
    grouped = (projector.reshape(patches, slot_count, per_slot, tile_size, tile_size),
               slot_ray.reshape(patches, slot_count).astype(jnp.int32),
               pixel_index.reshape(patches, slot_count, per_slot))

    def forward(running, pieces):
        tiles_here, rays_here, pixels_here = pieces
        gathered = volume[pixels_here].astype(jnp.float32)
        partial_value = jnp.einsum("sgrp,sgpc->src", tiles_here.astype(jnp.float32), gathered,
                             precision=lax.Precision.HIGHEST)
        return running.at[rays_here].add(partial_value), None

    projection = lax.scan(forward, jnp.zeros((ray_count, tile_size, slice_count), jnp.float32), grouped)[0]
    weights = weight_table[weight_index].astype(jnp.float32)
    residual = (weights[:, :, None] * (sinogram.astype(jnp.float32) - projection)).astype(jnp.bfloat16)

    def backward(running, pieces):
        totals, column_sum = running
        tiles_here, rays_here, pixels_here = pieces
        tiles_wide = tiles_here.astype(jnp.float32)
        spread = jnp.einsum("sgrp,src->sgpc", tiles_wide, residual[rays_here].astype(jnp.float32),
                            precision=lax.Precision.HIGHEST)
        flat_pixels = pixels_here.reshape(-1)
        totals = totals.at[flat_pixels].add(spread.reshape(-1, tile_size, slice_count))
        column_sum = column_sum.at[flat_pixels].add(jnp.sum(tiles_wide, axis=2).reshape(-1, tile_size))
        return (totals, column_sum), None

    start = (jnp.zeros((volume.shape[0], tile_size, slice_count), jnp.float32),
             jnp.zeros((volume.shape[0], tile_size), jnp.float32))
    carried = lax.scan(backward, start, grouped)[0]
    return volume.astype(jnp.float32) + carried[0] / carried[1][:, :, None]
```

```python
import functools
import math

import jax
import jax.numpy as jnp
from jax import lax
from jax.experimental import pallas as pl
from jax.experimental.pallas import tpu as pltpu
from jax.sharding import PartitionSpec as P

FULL = 32700.0
VMEM = pl.BlockSpec(memory_space=pltpu.VMEM)
SMEM = pl.BlockSpec(memory_space=pltpu.SMEM)
LIMIT = 40 * 2**20


def round_up(value, step):
    return -(-value // step) * step


def swap(value, axis, bits):
    size = lax.axis_size(axis)
    return lax.ppermute(value, axis, [(i, i ^ bits) for i in range(size)])


def pack(tile, out_ref, levels_ref, t):
    rows = tile.shape[0]
    top = jnp.maximum(jnp.max(jnp.abs(tile), axis=0, keepdims=True), 1e-30)
    level = jnp.ceil(jnp.log2(top))
    out_ref[pl.ds(pl.multiple_of(t * rows, rows), rows), :] = (
        jnp.round(tile * (FULL * jnp.exp2(-level))).astype(jnp.int32).astype(jnp.int16)
    )
    levels_ref[pl.ds(t, 1), :] = level


def unpack(ref, scale_ref, t, rows):
    block = ref[pl.ds(pl.multiple_of(t * rows, rows), rows), :]
    return block.astype(jnp.int32).astype(jnp.float32) * scale_ref[pl.ds(t, 1), :]


def cell_of(ray, zi, xi, tiles, outers, inners):
    owner = ray // tiles
    return ((owner % outers) ^ xi) * (inners * tiles) + ((owner // outers) ^ zi) * tiles + ray % tiles


def forward_kernel(
    outers, inners, tiles, pos_ref, ray_ref, pixel_ref, projector_ref, volume_ref, own_ref, *rest
):
    sends, (total, levels) = rest[:-2], rest[-2:]
    block, per_slot, rows, cols = projector_ref.shape
    step = pl.program_id(0)
    zi, xi = pos_ref[0], pos_ref[1]
    cells = outers * inners * tiles

    @pl.when(step == 0)
    def _():
        total[...] = jnp.zeros_like(total)

    @pl.loop(0, block)
    def _(i):
        s = step * block + i
        cell = cell_of(ray_ref[s], zi, xi, tiles, outers, inners)
        left = jnp.concatenate([projector_ref[i, g] for g in range(per_slot)], axis=1)
        right = jnp.concatenate([volume_ref[pixel_ref[s, g]] for g in range(per_slot)], axis=0)
        total[cell] += jnp.dot(left, right, preferred_element_type=jnp.float32)

    @pl.when(step == pl.num_programs(0) - 1)
    def _():
        own_ref[...] = total[: inners * tiles].reshape(own_ref.shape)
        levels[...] = jnp.zeros_like(levels)
        for c, send in enumerate(sends):
            base = (inners + c) * tiles

            @pl.loop(0, tiles)
            def _(t):
                pack(total[base + t], send, levels, t)

            send[tiles * rows :, :] = levels[...].astype(jnp.int32).astype(jnp.int16)


def forward(pos, slot_ray, slot_pixel, projector, volume, outers, inners, tiles):
    slots, per_slot, rows, cols = projector.shape
    slices = volume.shape[2]
    block = math.gcd(slots, 8)
    extra = round_up(tiles, 16)
    payload = jax.ShapeDtypeStruct((tiles * rows + extra, slices), jnp.int16)
    whole = lambda shape: pl.BlockSpec(shape, lambda i: (0,) * len(shape))
    count = (outers - 1) * inners
    return pl.pallas_call(
        functools.partial(forward_kernel, outers, inners, tiles),
        grid=(slots // block,),
        in_specs=[
            SMEM,
            SMEM,
            SMEM,
            pl.BlockSpec((block, per_slot, rows, cols), lambda i: (i, 0, 0, 0)),
            whole(volume.shape),
        ],
        out_specs=[whole((inners, tiles, rows, slices))] + [whole(payload.shape)] * count,
        out_shape=[jax.ShapeDtypeStruct((inners, tiles, rows, slices), jnp.float32)]
        + [payload] * count,
        scratch_shapes=[
            pltpu.VMEM((outers * inners * tiles, rows, slices), jnp.float32),
            pltpu.VMEM((extra, slices), jnp.float32),
        ],
        compiler_params=pltpu.CompilerParams(vmem_limit_bytes=LIMIT),
        cost_estimate=pl.CostEstimate(
            flops=2 * slots * per_slot * rows * cols * slices,
            bytes_accessed=projector.size * 2,
            transcendentals=0,
        ),
    )(pos, slot_ray, slot_pixel, projector, volume)


def scales(ref, tiles, rows):
    raw = ref[tiles * rows :, :].astype(jnp.int32).astype(jnp.float32)
    return jnp.exp2(raw) * (1.0 / FULL)


def combine_kernel(count, own_ref, *rest):
    arrived, out_ref, scale_refs, levels = (
        rest[:count],
        rest[count],
        rest[count + 1 : 2 * count + 1],
        rest[-1],
    )
    _, tiles, rows, _ = own_ref.shape
    levels[...] = jnp.zeros_like(levels)
    for ref, scale_ref in zip(arrived, scale_refs):
        scale_ref[...] = scales(ref, tiles, rows)

    @pl.loop(0, tiles)
    def _(t):
        tile = own_ref[0, t]
        for ref, scale_ref in zip(arrived, scale_refs):
            tile = tile + unpack(ref, scale_ref, t, rows)
        pack(tile, out_ref, levels, t)

    out_ref[tiles * rows :, :] = levels[...].astype(jnp.int32).astype(jnp.int16)


def combine(own, k, arrived):
    _, tiles, rows, slices = own.shape
    extra = round_up(tiles, 16)
    count = len(arrived)
    return pl.pallas_call(
        functools.partial(combine_kernel, count),
        grid=(1,),
        in_specs=[pl.BlockSpec((1, tiles, rows, slices), lambda i: (k, 0, 0, 0))] + [VMEM] * count,
        out_specs=VMEM,
        out_shape=jax.ShapeDtypeStruct((tiles * rows + extra, slices), jnp.int16),
        scratch_shapes=[pltpu.VMEM((extra, slices), jnp.float32)] * (count + 1),
        compiler_params=pltpu.CompilerParams(vmem_limit_bytes=LIMIT),
    )(own, *arrived)


def residual_kernel(count, table_ref, own_ref, sinogram_ref, index_ref, *rest):
    arrived, out_ref, scale_refs, weight = (
        rest[:count],
        rest[count],
        rest[count + 1 : 2 * count + 1],
        rest[-1],
    )
    _, tiles, rows, _ = own_ref.shape
    for ref, scale_ref in zip(arrived, scale_refs):
        scale_ref[...] = scales(ref, tiles, rows)
    looked = jnp.zeros(weight.shape, jnp.float32)
    for c in range(table_ref.shape[0]):
        looked = jnp.where(index_ref[...] == c, table_ref[c], looked)
    weight[...] = looked

    @pl.loop(0, tiles)
    def _(t):
        tile = own_ref[0, t]
        for ref, scale_ref in zip(arrived, scale_refs):
            tile = tile + unpack(ref, scale_ref, t, rows)
        gap = (sinogram_ref[t].astype(jnp.float32) - tile).T
        out_ref[t] = (weight[pl.ds(t, 1), :] * gap).astype(jnp.bfloat16)


def residual_of(table, own, sinogram, index, arrived):
    _, tiles, rows, slices = own.shape
    extra = round_up(tiles, 16)
    count = len(arrived)
    return pl.pallas_call(
        functools.partial(residual_kernel, count),
        grid=(1,),
        in_specs=[SMEM, pl.BlockSpec((1, tiles, rows, slices), lambda i: (0, 0, 0, 0)), VMEM, VMEM]
        + [VMEM] * count,
        out_specs=VMEM,
        out_shape=jax.ShapeDtypeStruct((tiles, slices, rows), jnp.bfloat16),
        scratch_shapes=[pltpu.VMEM((extra, slices), jnp.float32)] * count
        + [pltpu.VMEM((tiles, rows), jnp.float32)],
        compiler_params=pltpu.CompilerParams(vmem_limit_bytes=LIMIT),
    )(table, own, sinogram, index, *arrived)


def column_kernel(pixel_ref, projector_ref, out_ref):
    block, per_slot, rows, cols = projector_ref.shape
    step = pl.program_id(0)

    @pl.when(step == 0)
    def _():
        out_ref[...] = jnp.zeros_like(out_ref)

    @pl.loop(0, block)
    def _(i):
        for g in range(per_slot):
            column = jnp.sum(projector_ref[i, g].astype(jnp.float32), axis=0, keepdims=True)
            out_ref[pixel_ref[step * block + i, g]] += column


def column_sums(slot_pixel, projector, patch_tiles):
    slots, per_slot, rows, cols = projector.shape
    block = math.gcd(slots, 8)
    return pl.pallas_call(
        column_kernel,
        grid=(slots // block,),
        in_specs=[SMEM, pl.BlockSpec((block, per_slot, rows, cols), lambda i: (i, 0, 0, 0))],
        out_specs=pl.BlockSpec((patch_tiles, 1, cols), lambda i: (0, 0, 0)),
        out_shape=jax.ShapeDtypeStruct((patch_tiles, 1, cols), jnp.float32),
        compiler_params=pltpu.CompilerParams(vmem_limit_bytes=LIMIT),
        cost_estimate=pl.CostEstimate(
            flops=2 * projector.size, bytes_accessed=projector.size * 2, transcendentals=0
        ),
    )(slot_pixel, projector)


def backward_kernel(
    outers, inners, pos_ref, ray_ref, pixel_ref, projector_ref, volume_ref, column_ref, *rest
):
    chunks, (out_ref, held, total) = rest[:-3], rest[-3:]
    block, per_slot, rows, cols = projector_ref.shape
    tiles = chunks[0].shape[0]
    step = pl.program_id(0)
    zi, xi = pos_ref[0], pos_ref[1]

    @pl.when(step == 0)
    def _():
        total[...] = jnp.zeros_like(total)
        for c, chunk in enumerate(chunks):
            held[c * tiles : (c + 1) * tiles] = chunk[...]

    @pl.loop(0, block)
    def _(i):
        s = step * block + i
        cell = cell_of(ray_ref[s], zi, xi, tiles, outers, inners)
        right = jnp.concatenate([projector_ref[i, g] for g in range(per_slot)], axis=1)
        spread = jnp.dot(held[cell], right, preferred_element_type=jnp.float32)
        for g in range(per_slot):
            total[pixel_ref[s, g]] += spread[:, g * cols : (g + 1) * cols]

    @pl.when(step == pl.num_programs(0) - 1)
    def _():
        @pl.loop(0, total.shape[0])
        def _(q):
            out_ref[q] = volume_ref[q].astype(jnp.float32) + (total[q] / column_ref[q]).T


def backward(pos, slot_ray, slot_pixel, projector, volume, columns, chunks, outers, inners):
    slots, per_slot, rows, cols = projector.shape
    tiles = chunks[0].shape[0]
    patch_tiles, _, slices = volume.shape
    block = math.gcd(slots, 8)
    whole = lambda shape: pl.BlockSpec(shape, lambda i: (0,) * len(shape))
    return pl.pallas_call(
        functools.partial(backward_kernel, outers, inners),
        grid=(slots // block,),
        in_specs=[
            SMEM,
            SMEM,
            SMEM,
            pl.BlockSpec((block, per_slot, rows, cols), lambda i: (i, 0, 0, 0)),
            whole(volume.shape),
            whole(columns.shape),
        ]
        + [whole(chunks[0].shape)] * len(chunks),
        out_specs=whole(volume.shape),
        out_shape=jax.ShapeDtypeStruct(volume.shape, jnp.float32),
        scratch_shapes=[
            pltpu.VMEM((len(chunks) * tiles, slices, rows), jnp.bfloat16),
            pltpu.VMEM((patch_tiles, slices, cols), jnp.float32),
        ],
        compiler_params=pltpu.CompilerParams(vmem_limit_bytes=LIMIT),
        cost_estimate=pl.CostEstimate(
            flops=2 * slots * per_slot * rows * cols * slices,
            bytes_accessed=projector.size * 2,
            transcendentals=0,
        ),
    )(pos, slot_ray, slot_pixel, projector, volume, columns, *chunks)


def dense_plan(volume, projector, slot_ray, slot_pixel, sinogram, weight_index, weight_table):
    inners = lax.axis_size("inner")
    outers = lax.axis_size("outer")
    tiles = sinogram.shape[0]
    pos = jnp.stack([lax.axis_index("inner"), lax.axis_index("outer")]).astype(jnp.int32)
    own, *sends = forward(pos, slot_ray, slot_pixel, projector, volume, outers, inners, tiles)
    arrived = {k: [] for k in range(inners)}
    for k in reversed(range(inners)):
        for j in range(1, outers):
            arrived[k].append(swap(sends[(j - 1) * inners + k], "outer", j))
    columns = column_sums(slot_pixel, projector, volume.shape[0])
    live = list(range(inners))
    bit = 1
    while bit < inners:
        for k in reversed([k for k in live if k & bit]):
            arrived[k ^ bit].append(swap(combine(own, k, arrived[k]), "inner", bit))
        live = [k for k in live if not k & bit]
        bit *= 2
    residual = residual_of(
        weight_table.astype(jnp.float32), own, sinogram, weight_index, arrived[0]
    )
    held = {0: residual}
    while bit > 1:
        bit //= 2
        for k in sorted(held):
            held[k ^ bit] = swap(held[k], "inner", bit)
    chunks = [held[k] for k in range(inners)]
    for j in range(1, outers):
        chunks += [swap(held[k], "outer", j) for k in range(inners)]
    return backward(
        pos, slot_ray, slot_pixel, projector, volume, columns, chunks, outers, inners
    )


def slot_plan(volume, projector, slot_ray, slot_pixel, sinogram, weight_index, weight_table):
    inners = lax.axis_size("inner")
    outers = lax.axis_size("outer")
    slot_count = projector.shape[0]
    per_slot = projector.shape[1]
    tile_rows = projector.shape[2]
    tile_cols = projector.shape[3]
    patch_tiles = volume.shape[0]
    slice_count = volume.shape[2]
    owned_rows = sinogram.shape[0]
    band_rows = owned_rows * outers
    capacity = 2 * slot_count // inners
    cell_count = inners * capacity
    target = slot_ray // band_rows
    offset = slot_ray % band_rows
    same_target = target[:, None] == target[None, :]
    earlier = jnp.arange(slot_count)[:, None] > jnp.arange(slot_count)[None, :]
    slot_rank = jnp.sum(jnp.logical_and(same_target, earlier), axis=1)
    position = target * capacity + slot_rank
    partial_value = jnp.zeros((slot_count, tile_rows, slice_count), jnp.float32)
    for column in range(per_slot):
        pixels = volume[slot_pixel[:, column]]
        partial_value = partial_value + jnp.einsum(
            "srp,spc->src", projector[:, column], pixels, preferred_element_type=jnp.float32
        )
    outgoing = (
        jnp.zeros((cell_count, tile_rows, slice_count), jnp.float32).at[position].set(partial_value)
    )
    labels = jnp.full((cell_count,), -1.0, jnp.float32).at[position].set(offset.astype(jnp.float32))
    arrived, arrived_rows = (
        lax.all_to_all(
            outgoing.reshape(inners, capacity, tile_rows, slice_count),
            "inner",
            split_axis=0,
            concat_axis=0,
            tiled=True,
        ),
        lax.all_to_all(
            labels.reshape(inners, capacity), "inner", split_axis=0, concat_axis=0, tiled=True
        ),
    )
    selector = (
        jnp.arange(band_rows, dtype=jnp.float32)[:, None] == arrived_rows.reshape(1, cell_count)
    ).astype(jnp.float32)
    block_sums = jnp.dot(
        selector,
        arrived.reshape(cell_count, tile_rows * slice_count),
        precision=lax.Precision.HIGHEST,
    ).reshape(band_rows, tile_rows, slice_count)
    classes = weight_table.shape[0]
    lookup = weight_index[:, :, None] == jnp.arange(classes)[None, None, :]
    weights = jnp.sum(
        jnp.where(lookup, weight_table[None, None, :], jnp.zeros((), weight_table.dtype)), axis=2
    )
    own_sums = lax.psum_scatter(block_sums, "outer", scatter_dimension=0, tiled=True)
    own_residual = (
        weights.astype(jnp.float32)[:, :, None] * (sinogram.astype(jnp.float32) - own_sums)
    ).astype(jnp.bfloat16)
    residual = lax.all_gather(own_residual, "outer", axis=0, tiled=True)
    picked = jnp.dot(
        selector.T.astype(jnp.bfloat16),
        residual.reshape(band_rows, tile_rows * slice_count),
        preferred_element_type=jnp.float32,
    ).astype(jnp.bfloat16)
    returned = lax.all_to_all(
        picked.reshape(inners, capacity, tile_rows, slice_count),
        "inner",
        split_axis=0,
        concat_axis=0,
        tiled=True,
    )
    slot_residual = returned.reshape(cell_count, tile_rows, slice_count)[position]
    owners = jnp.arange(patch_tiles)
    backward_sum = jnp.zeros((patch_tiles, tile_cols, slice_count), jnp.float32)
    column_sum = jnp.zeros((patch_tiles, tile_cols), jnp.float32)
    for column in range(per_slot):
        member = (owners[:, None] == slot_pixel[None, :, column]).astype(jnp.float32)
        spread = jnp.einsum(
            "srp,src->spc", projector[:, column], slot_residual, preferred_element_type=jnp.float32
        )
        backward_sum = backward_sum + jnp.einsum(
            "ts,spc->tpc", member, spread, precision=lax.Precision.HIGHEST
        )
        column_sum = column_sum + jnp.dot(
            member,
            jnp.sum(projector[:, column], axis=1, dtype=jnp.float32),
            precision=lax.Precision.HIGHEST,
        )
    return volume.astype(jnp.float32) + backward_sum / column_sum[:, :, None]


def on_device(volume, projector, slot_ray, slot_pixel, sinogram, weight_index, weight_table):
    inners = lax.axis_size("inner")
    outers = lax.axis_size("outer")
    capacity = 2 * slot_ray.shape[0] // inners
    powers = inners & (inners - 1) == 0 and outers & (outers - 1) == 0
    plan = dense_plan if powers and sinogram.shape[0] * outers <= capacity else slot_plan
    return plan(volume, projector, slot_ray, slot_pixel, sinogram, weight_index, weight_table)


def solution(mesh):
    in_specs = (
        P(("group", "inner", "outer"), None, "cuts"),
        P(("inner", "outer"), None, None, None),
        P(("inner", "outer")),
        P(("inner", "outer"), None),
        P(("group", "inner", "outer"), None, "cuts"),
        P(("group", "inner", "outer"), None),
        P(),
    )
    out_specs = P(("group", "inner", "outer"), None, "cuts")
    return jax.shard_map(
        on_device, mesh=mesh, in_specs=in_specs, out_specs=out_specs, check_vma=False
    )
```

```python
import functools
import math

import jax
import jax.numpy as jnp
from jax import lax
from jax.experimental import pallas as pl
from jax.experimental.pallas import tpu as pltpu
from jax.sharding import PartitionSpec as P

FULL = 32700.0
UNROLL = 4
VMEM = pl.BlockSpec(memory_space=pltpu.VMEM)
SMEM = pl.BlockSpec(memory_space=pltpu.SMEM)
HBM = pl.BlockSpec(memory_space=pltpu.HBM)
ANY = pl.BlockSpec(memory_space=pl.ANY)
QUICK = pl.CostEstimate(flops=1, bytes_accessed=1, transcendentals=0)
PARAMS = pltpu.CompilerParams(vmem_limit_bytes=24 * 2**20)


def round_up(value, step):
    return -(-value // step) * step


def swap(value, axis, bits):
    size = lax.axis_size(axis)
    return lax.ppermute(value, axis, [(i, i ^ bits) for i in range(size)])


def pack(tile, out_ref, levels_ref, t):
    rows = tile.shape[0]
    top = jnp.maximum(jnp.max(jnp.abs(tile), axis=0, keepdims=True), 1e-30)
    level = jnp.ceil(jnp.log2(top))
    out_ref[t * rows : (t + 1) * rows, :] = (
        jnp.round(tile * (FULL * jnp.exp2(-level))).astype(jnp.int32).astype(jnp.int16)
    )
    levels_ref[t : t + 1, :] = level


def unpack(ref, scale, t, rows):
    block = ref[t * rows : (t + 1) * rows, :]
    return block.astype(jnp.int32).astype(jnp.float32) * scale[t : t + 1, :]


def scales(ref, tiles, rows):
    raw = ref[tiles * rows :, :].astype(jnp.int32).astype(jnp.float32)
    return jnp.exp2(raw) * (1.0 / FULL)


def payload_of(tiles, rows, slices):
    return jax.ShapeDtypeStruct((tiles * rows + round_up(tiles, 16), slices), jnp.int16)


def split(value, size):
    if size & (size - 1) == 0:
        return lax.shift_right_logical(value, size.bit_length() - 1), value & (size - 1)
    return lax.div(value, size), lax.rem(value, size)


def cell_of(ray, zi, xi, tiles, outers, inners):
    owner, tile = split(ray, tiles)
    inner, outer = split(owner, outers)
    return ((outer ^ xi) * inners + (inner ^ zi)) * tiles + tile


def list_slots(cell_ref, tiles, groups, slot_list):
    slots = cell_ref.shape[0]

    def look(s, count):
        slot_list[count] = s
        cell = cell_ref[s]
        hit = jnp.bool_(False)
        for group in groups:
            hit = hit | ((cell >= group * tiles) & (cell < (group + 1) * tiles))
        return count + hit.astype(jnp.int32)

    return lax.fori_loop(0, slots, look, jnp.int32(0), unroll=4)


def project(count, base, spare, slot_list, cell_ref, pixel_ref, projector_ref, volume_ref, total):
    per_slot = projector_ref.shape[1]

    @pl.loop(0, (count + UNROLL - 1) // UNROLL)
    def _(i):
        parts, places = [], []
        for u in range(UNROLL):
            at = i * UNROLL + u
            real = at < count
            s = jnp.where(real, slot_list[at], 0)
            left = jnp.concatenate([projector_ref[s, g] for g in range(per_slot)], axis=1)
            right = jnp.concatenate([volume_ref[pixel_ref[g, s]] for g in range(per_slot)], axis=0)
            parts.append(jnp.dot(left, right, preferred_element_type=jnp.float32))
            places.append(jnp.where(real, cell_ref[s] - base, spare))
        for place, part in zip(places, parts):
            total[place] += part


def send_out(total, base, tiles, arrived, send, levels):
    rows = total.shape[1]
    levels[...] = jnp.zeros_like(levels)
    factors = [scales(ref, tiles, rows) for ref in arrived]
    for t in range(tiles):
        tile = total[base + t]
        for ref, factor in zip(arrived, factors):
            tile = tile + unpack(ref, factor, t, rows)
        pack(tile, send, levels, t)
    send[tiles * rows :, :] = levels[...].astype(jnp.int32).astype(jnp.int16)


def first_kernel(
    sizes, group, pos_ref, ray_hbm, pixel_hbm, projector_hbm, volume_hbm,
    send, projector_ref, volume_ref, cell_ref, ray_ref, pixel_ref, slot_list, total, levels, sems,
):
    outers, inners, tiles = sizes
    pairs = [
        (ray_hbm, ray_ref),
        (projector_hbm, projector_ref),
        (volume_hbm, volume_ref),
        (pixel_hbm, pixel_ref),
    ]
    copies = [
        pltpu.make_async_copy(source, target, sems.at[i]) for i, (source, target) in enumerate(pairs)
    ]
    for copy in copies:
        copy.start()
    total[...] = jnp.zeros_like(total)
    copies[0].wait()
    zi, xi = pos_ref[0], pos_ref[1]

    @pl.loop(0, ray_ref.shape[0], unroll=4)
    def _(s):
        cell_ref[s] = cell_of(ray_ref[s], zi, xi, tiles, outers, inners)

    count = list_slots(cell_ref, tiles, [group], slot_list)
    for copy in copies[1:]:
        copy.wait()
    project(
        count, group * tiles, tiles, slot_list, cell_ref, pixel_ref, projector_ref, volume_ref, total
    )
    send_out(total, 0, tiles, [], send, levels)


def hold(value):
    return pltpu.with_memory_space_constraint(value, pltpu.HBM)


def first_send(pos, slot_ray, pixel, projector, volume, sizes, group):
    slots, per_slot, rows, cols = projector.shape
    tiles = sizes[2]
    slices = volume.shape[2]
    return pl.pallas_call(
        functools.partial(first_kernel, sizes, group),
        in_specs=[SMEM, HBM, HBM, HBM, HBM],
        out_specs=[VMEM, VMEM, VMEM, SMEM],
        out_shape=[
            payload_of(tiles, rows, slices),
            jax.ShapeDtypeStruct(projector.shape, projector.dtype),
            jax.ShapeDtypeStruct(volume.shape, volume.dtype),
            jax.ShapeDtypeStruct(slot_ray.shape, jnp.int32),
        ],
        scratch_shapes=[
            pltpu.SMEM(slot_ray.shape, jnp.int32),
            pltpu.SMEM(pixel.shape, jnp.int32),
            pltpu.SMEM((slots + UNROLL,), jnp.int32),
            pltpu.VMEM((tiles + 1, rows, slices), jnp.float32),
            pltpu.VMEM((round_up(tiles, 16), slices), jnp.float32),
            pltpu.SemaphoreType.DMA((4,)),
        ],
        compiler_params=PARAMS,
        cost_estimate=QUICK,
    )(pos, hold(slot_ray), hold(pixel), hold(projector), hold(volume))


def next_kernel(
    tiles, group, count, cell_ref, pixel_ref, projector_ref, volume_ref, after, *rest
):
    arrived, (send, slot_list, total, levels) = rest[:count], rest[count:]
    total[...] = jnp.zeros_like(total)
    count = list_slots(cell_ref, tiles, [group], slot_list)
    project(
        count, group * tiles, tiles, slot_list, cell_ref, pixel_ref, projector_ref, volume_ref, total
    )
    send_out(total, 0, tiles, arrived, send, levels)


def next_send(cells, pixel, projector, volume, tiles, group, arrived, after):
    slots, per_slot, rows, cols = projector.shape
    slices = volume.shape[2]
    return pl.pallas_call(
        functools.partial(next_kernel, tiles, group, len(arrived)),
        in_specs=[SMEM, SMEM, VMEM, VMEM, ANY] + [VMEM] * len(arrived),
        out_specs=VMEM,
        out_shape=payload_of(tiles, rows, slices),
        scratch_shapes=[
            pltpu.SMEM((slots + UNROLL,), jnp.int32),
            pltpu.VMEM((tiles + 1, rows, slices), jnp.float32),
            pltpu.VMEM((round_up(tiles, 16), slices), jnp.float32),
        ],
        compiler_params=PARAMS,
        cost_estimate=QUICK,
    )(cells, pixel, projector, volume, after, *arrived)


def own_kernel(
    inners, tiles, cell_ref, pixel_ref, projector_ref, volume_ref, after, own_ref, slot_list
):
    own_ref[...] = jnp.zeros_like(own_ref)
    count = list_slots(cell_ref, inners * tiles, [0], slot_list)
    project(
        count, 0, inners * tiles, slot_list, cell_ref, pixel_ref, projector_ref, volume_ref, own_ref
    )


def own_sums(cells, pixel, projector, volume, inners, tiles, after):
    slots, per_slot, rows, cols = projector.shape
    slices = volume.shape[2]
    return pl.pallas_call(
        functools.partial(own_kernel, inners, tiles),
        in_specs=[SMEM, SMEM, VMEM, VMEM, ANY],
        out_specs=VMEM,
        out_shape=jax.ShapeDtypeStruct((inners * tiles + 1, rows, slices), jnp.float32),
        scratch_shapes=[pltpu.SMEM((slots + UNROLL,), jnp.int32)],
        compiler_params=PARAMS,
        cost_estimate=QUICK,
    )(cells, pixel, projector, volume, after)


def combine_kernel(k, tiles, count, own_ref, after, *rest):
    arrived, (out_ref, levels) = rest[:count], rest[count:]
    send_out(own_ref, k * tiles, tiles, arrived, out_ref, levels)


def combine(own, k, tiles, arrived, after):
    _, rows, slices = own.shape
    count = len(arrived)
    return pl.pallas_call(
        functools.partial(combine_kernel, k, tiles, count),
        in_specs=[VMEM, ANY] + [VMEM] * count,
        out_specs=VMEM,
        out_shape=payload_of(tiles, rows, slices),
        scratch_shapes=[pltpu.VMEM((round_up(tiles, 16), slices), jnp.float32)],
        compiler_params=PARAMS,
        cost_estimate=QUICK,
    )(own, after, *arrived)


def weight_kernel(table_ref, index_ref, after, out_ref):
    looked = jnp.zeros(index_ref.shape, jnp.float32)
    for c in range(table_ref.shape[0]):
        looked = jnp.where(index_ref[...] == c, table_ref[c], looked)
    for t in range(index_ref.shape[0]):
        wide = jnp.broadcast_to(looked[t : t + 1, :], (out_ref.shape[2], out_ref.shape[1]))
        out_ref[t] = wide.T.astype(jnp.bfloat16)


def ray_weights(table, index, slices, after):
    tiles, rows = index.shape
    return pl.pallas_call(
        weight_kernel,
        in_specs=[SMEM, VMEM, ANY],
        out_specs=VMEM,
        out_shape=jax.ShapeDtypeStruct((tiles, rows, slices), jnp.bfloat16),
        compiler_params=PARAMS,
        cost_estimate=QUICK,
    )(table.astype(jnp.float32), index, after)


def residual_kernel(count, own_ref, sinogram_ref, weight_ref, *rest):
    arrived, out_ref = rest[:count], rest[count]
    tiles, rows, _ = sinogram_ref.shape
    factors = [scales(ref, tiles, rows) for ref in arrived]
    for t in range(tiles):
        tile = own_ref[t]
        for ref, factor in zip(arrived, factors):
            tile = tile + unpack(ref, factor, t, rows)
        gap = sinogram_ref[t].astype(jnp.float32) - tile
        out_ref[t] = (weight_ref[t].astype(jnp.float32) * gap).astype(jnp.bfloat16)


def residual_of(own, sinogram, weights, arrived):
    return pl.pallas_call(
        functools.partial(residual_kernel, len(arrived)),
        in_specs=[VMEM, VMEM, VMEM] + [VMEM] * len(arrived),
        out_specs=VMEM,
        out_shape=jax.ShapeDtypeStruct(sinogram.shape, jnp.bfloat16),
        compiler_params=PARAMS,
        cost_estimate=QUICK,
    )(own, sinogram, weights, *arrived)


def column_kernel(pixel_ref, projector_ref, after, out_ref):
    slots, per_slot, rows, cols = projector_ref.shape
    out_ref[...] = jnp.zeros_like(out_ref)

    @pl.loop(0, slots)
    def _(s):
        for g in range(per_slot):
            column = jnp.sum(projector_ref[s, g].astype(jnp.float32), axis=0, keepdims=True)
            out_ref[pixel_ref[g, s]] += column


def column_sums(pixel, projector, patch_tiles, after):
    slots, per_slot, rows, cols = projector.shape
    return pl.pallas_call(
        column_kernel,
        in_specs=[SMEM, VMEM, ANY],
        out_specs=VMEM,
        out_shape=jax.ShapeDtypeStruct((patch_tiles, 1, cols), jnp.float32),
        compiler_params=PARAMS,
        cost_estimate=QUICK,
    )(pixel, projector, after)


def spread_kernel(groups, begin, cell_ref, pixel_ref, projector_ref, *rest):
    if not begin:
        before, rest = rest[0], rest[1:]
    chunks, (total, slot_list, held) = rest[: len(groups)], rest[len(groups) :]
    slots, per_slot, rows, cols = projector_ref.shape
    tiles = chunks[0].shape[0]
    patch_tiles = total.shape[0] - 1
    for group, chunk in zip(groups, chunks):
        held[group * tiles : (group + 1) * tiles] = chunk[...]
    if begin:
        total[...] = jnp.zeros_like(total)
    else:
        total[...] = before[...]
    count = list_slots(cell_ref, tiles, groups, slot_list)

    @pl.loop(0, (count + 1) // 2)
    def _(i):
        parts, places = [], []
        for u in range(2):
            real = i * 2 + u < count
            s = jnp.where(real, slot_list[i * 2 + u], slot_list[0])
            right = jnp.concatenate([projector_ref[s, g] for g in range(per_slot)], axis=1)
            parts.append(
                lax.dot_general(
                    held[cell_ref[s]], right, (((0,), (0,)), ((), ())), preferred_element_type=jnp.float32
                )
            )
            places.append([jnp.where(real, pixel_ref[g, s], patch_tiles) for g in range(per_slot)])
        for part, place in zip(parts, places):
            for g in range(per_slot):
                total[place[g]] += part[:, g * cols : (g + 1) * cols]


def spread(cells, pixel, projector, all_groups, groups, chunks, patch_tiles, before):
    slots, per_slot, rows, cols = projector.shape
    tiles, _, slices = chunks[0].shape
    begin = before is None
    return pl.pallas_call(
        functools.partial(spread_kernel, groups, begin),
        in_specs=[SMEM, SMEM, VMEM] + [VMEM] * (len(chunks) + (not begin)),
        out_specs=VMEM,
        out_shape=jax.ShapeDtypeStruct((patch_tiles + 1, slices, cols), jnp.float32),
        scratch_shapes=[
            pltpu.SMEM((slots + UNROLL,), jnp.int32),
            pltpu.VMEM((all_groups * tiles, rows, slices), jnp.bfloat16),
        ],
        compiler_params=PARAMS,
        cost_estimate=QUICK,
    )(cells, pixel, projector, *([] if begin else [before]), *chunks)


def update_kernel(volume_ref, column_ref, total_ref, out_ref):
    for q in range(out_ref.shape[0]):
        out_ref[q] = volume_ref[q].astype(jnp.float32) + (total_ref[q] / column_ref[q]).T


def update(volume, columns, total):
    return pl.pallas_call(
        update_kernel,
        in_specs=[VMEM, VMEM, VMEM],
        out_specs=VMEM,
        out_shape=jax.ShapeDtypeStruct(volume.shape, jnp.float32),
        compiler_params=PARAMS,
        cost_estimate=QUICK,
    )(volume, columns, total)


def gate(value, after):
    return pl.pallas_call(
        lambda value_ref, after_ref, out_ref: None,
        in_specs=[VMEM, VMEM],
        out_specs=VMEM,
        out_shape=jax.ShapeDtypeStruct(value.shape, value.dtype),
        input_output_aliases={0: 0},
        compiler_params=PARAMS,
        cost_estimate=QUICK,
    )(value, after)


def dense_plan(volume, projector, slot_ray, slot_pixel, sinogram, weight_index, weight_table):
    inners = lax.axis_size("inner")
    outers = lax.axis_size("outer")
    tiles = sinogram.shape[0]
    patch_tiles, _, slices = volume.shape
    sizes = (outers, inners, tiles)
    pos = jnp.stack([lax.axis_index("inner"), lax.axis_index("outer")]).astype(jnp.int32)
    pixel = slot_pixel.T

    turns = sorted(range(inners), key=lambda k: (bin(k).count("1"), k), reverse=True)
    far = [k for k in turns if k > 1]
    others = range(1, outers)
    arrived = {g: [] for g in range(outers * inners)}
    sends = []
    for k in far[:1]:
        sends += [(j * inners + k, "outer", j) for j in others]
    if inners > 1:
        sends += [(j * inners + 1, "inner", 1) for j in others]
    for k in far[1:]:
        sends += [(j * inners + k, "outer", j) for j in others]
    cells = None
    for group, axis, bits in sends:
        if cells is None:
            after, projector, volume, cells = first_send(
                pos, slot_ray, pixel, projector, volume, sizes, group
            )
        else:
            after = next_send(cells, pixel, projector, volume, tiles, group, [], after)
        place = group ^ 1 if axis == "inner" else group % inners
        arrived[place].append(swap(after, axis, bits))
    after = own = own_sums(cells, pixel, projector, volume, inners, tiles, after)
    for i, k in enumerate(far):
        bit = k & -k
        after = combine(own, k, tiles, arrived[k], after)
        arrived[k ^ bit].append(swap(after, "inner", bit))
        if i == 0:
            for j in others:
                group = j * inners
                after = next_send(
                    cells, pixel, projector, volume, tiles, group, arrived[group], after
                )
                arrived[0].append(swap(after, "outer", j))
    after = combine(own, 1, tiles, [], after)
    arrived[0].append(swap(after, "inner", 1))
    weights = ray_weights(weight_table, weight_index, slices, after)
    columns = column_sums(pixel, projector, patch_tiles, weights)
    residual = residual_of(own, sinogram, weights, arrived[0])

    turns = turns[::-1]
    chunks = {0: residual}
    total = None

    def add(groups):
        return spread(
            cells, pixel, projector, outers * inners, groups, [chunks[g] for g in groups], patch_tiles, total
        )

    bit = inners // 2
    while bit:
        chunks[bit] = swap(residual, "inner", bit)
        bit //= 2
    for j in others:
        chunks[j * inners] = swap(residual, "outer", j)
        chunks[j * inners + 1] = swap(chunks[j * inners], "inner", 1)
    total = add([0, 1] + [j * inners for j in others])
    waiting = [j * inners + 1 for j in others]
    for k in turns[2:]:
        chunks[k] = gate(chunks[k], total)
        bit = (k & -k) // 2
        while bit:
            chunks[k ^ bit] = swap(chunks[k], "inner", bit)
            bit //= 2
        for j in others:
            chunks[j * inners + k] = swap(chunks[k], "outer", j)
        total = add([k] + waiting)
        waiting = [j * inners + k for j in others]
    total = add(waiting)
    return update(volume, columns, total)


def slot_plan(volume, projector, slot_ray, slot_pixel, sinogram, weight_index, weight_table):
    inners = lax.axis_size("inner")
    outers = lax.axis_size("outer")
    slot_count = projector.shape[0]
    per_slot = projector.shape[1]
    tile_rows = projector.shape[2]
    tile_cols = projector.shape[3]
    patch_tiles = volume.shape[0]
    slice_count = volume.shape[2]
    owned_rows = sinogram.shape[0]
    band_rows = owned_rows * outers
    capacity = 2 * slot_count // inners
    cell_count = inners * capacity
    target = slot_ray // band_rows
    offset = slot_ray % band_rows
    same_target = target[:, None] == target[None, :]
    earlier = jnp.arange(slot_count)[:, None] > jnp.arange(slot_count)[None, :]
    slot_rank = jnp.sum(jnp.logical_and(same_target, earlier), axis=1)
    position = target * capacity + slot_rank
    partial_value = jnp.zeros((slot_count, tile_rows, slice_count), jnp.float32)
    for column in range(per_slot):
        pixels = volume[slot_pixel[:, column]]
        partial_value = partial_value + jnp.einsum(
            "srp,spc->src", projector[:, column], pixels, preferred_element_type=jnp.float32
        )
    outgoing = (
        jnp.zeros((cell_count, tile_rows, slice_count), jnp.float32).at[position].set(partial_value)
    )
    labels = jnp.full((cell_count,), -1.0, jnp.float32).at[position].set(offset.astype(jnp.float32))
    arrived, arrived_rows = (
        lax.all_to_all(
            outgoing.reshape(inners, capacity, tile_rows, slice_count),
            "inner",
            split_axis=0,
            concat_axis=0,
            tiled=True,
        ),
        lax.all_to_all(
            labels.reshape(inners, capacity), "inner", split_axis=0, concat_axis=0, tiled=True
        ),
    )
    selector = (
        jnp.arange(band_rows, dtype=jnp.float32)[:, None] == arrived_rows.reshape(1, cell_count)
    ).astype(jnp.float32)
    block_sums = jnp.dot(
        selector,
        arrived.reshape(cell_count, tile_rows * slice_count),
        precision=lax.Precision.HIGHEST,
    ).reshape(band_rows, tile_rows, slice_count)
    classes = weight_table.shape[0]
    lookup = weight_index[:, :, None] == jnp.arange(classes)[None, None, :]
    weights = jnp.sum(
        jnp.where(lookup, weight_table[None, None, :], jnp.zeros((), weight_table.dtype)), axis=2
    )
    own_sums = lax.psum_scatter(block_sums, "outer", scatter_dimension=0, tiled=True)
    own_residual = (
        weights.astype(jnp.float32)[:, :, None] * (sinogram.astype(jnp.float32) - own_sums)
    ).astype(jnp.bfloat16)
    residual = lax.all_gather(own_residual, "outer", axis=0, tiled=True)
    picked = jnp.dot(
        selector.T.astype(jnp.bfloat16),
        residual.reshape(band_rows, tile_rows * slice_count),
        preferred_element_type=jnp.float32,
    ).astype(jnp.bfloat16)
    returned = lax.all_to_all(
        picked.reshape(inners, capacity, tile_rows, slice_count),
        "inner",
        split_axis=0,
        concat_axis=0,
        tiled=True,
    )
    slot_residual = returned.reshape(cell_count, tile_rows, slice_count)[position]
    owners = jnp.arange(patch_tiles)
    backward_sum = jnp.zeros((patch_tiles, tile_cols, slice_count), jnp.float32)
    column_sum = jnp.zeros((patch_tiles, tile_cols), jnp.float32)
    for column in range(per_slot):
        member = (owners[:, None] == slot_pixel[None, :, column]).astype(jnp.float32)
        spread = jnp.einsum(
            "srp,src->spc", projector[:, column], slot_residual, preferred_element_type=jnp.float32
        )
        backward_sum = backward_sum + jnp.einsum(
            "ts,spc->tpc", member, spread, precision=lax.Precision.HIGHEST
        )
        column_sum = column_sum + jnp.dot(
            member,
            jnp.sum(projector[:, column], axis=1, dtype=jnp.float32),
            precision=lax.Precision.HIGHEST,
        )
    return volume.astype(jnp.float32) + backward_sum / column_sum[:, :, None]


def on_device(volume, projector, slot_ray, slot_pixel, sinogram, weight_index, weight_table):
    inners = lax.axis_size("inner")
    outers = lax.axis_size("outer")
    capacity = 2 * slot_ray.shape[0] // inners
    powers = inners & (inners - 1) == 0 and outers & (outers - 1) == 0 and inners > 1 < outers
    plan = dense_plan if powers and sinogram.shape[0] * outers <= capacity else slot_plan
    return plan(volume, projector, slot_ray, slot_pixel, sinogram, weight_index, weight_table)


def solution(mesh):
    in_specs = (
        P(("group", "inner", "outer"), None, "cuts"),
        P(("inner", "outer"), None, None, None),
        P(("inner", "outer")),
        P(("inner", "outer"), None),
        P(("group", "inner", "outer"), None, "cuts"),
        P(("group", "inner", "outer"), None),
        P(),
    )
    out_specs = P(("group", "inner", "outer"), None, "cuts")
    return jax.shard_map(
        on_device, mesh=mesh, in_specs=in_specs, out_specs=out_specs, check_vma=False
    )
```

```python
import functools
import math

import jax
import jax.numpy as jnp
from jax import lax
from jax.experimental import pallas as pl
from jax.experimental.pallas import tpu as pltpu
from jax.sharding import PartitionSpec as P

FULL = 32700.0
UNROLL = 4
LATER = True
EARLY = False
VMEM = pl.BlockSpec(memory_space=pltpu.VMEM)
SMEM = pl.BlockSpec(memory_space=pltpu.SMEM)
HBM = pl.BlockSpec(memory_space=pltpu.HBM)
ANY = pl.BlockSpec(memory_space=pl.ANY)
QUICK = pl.CostEstimate(flops=1, bytes_accessed=1, transcendentals=0)
PARAMS = pltpu.CompilerParams(vmem_limit_bytes=24 * 2**20)


def round_up(value, step):
    return -(-value // step) * step


def swap(value, axis, bits):
    size = lax.axis_size(axis)
    return lax.ppermute(value, axis, [(i, i ^ bits) for i in range(size)])


def pack(tile, out_ref, levels_ref, t):
    rows = tile.shape[0]
    top = jnp.maximum(jnp.max(jnp.abs(tile), axis=0, keepdims=True), 1e-30)
    level = jnp.ceil(jnp.log2(top))
    out_ref[t * rows : (t + 1) * rows, :] = (
        jnp.round(tile * (FULL * jnp.exp2(-level))).astype(jnp.int32).astype(jnp.int16)
    )
    levels_ref[t : t + 1, :] = level


def unpack(ref, scale, t, rows):
    block = ref[t * rows : (t + 1) * rows, :]
    return block.astype(jnp.int32).astype(jnp.float32) * scale[t : t + 1, :]


def scales(ref, tiles, rows):
    raw = ref[tiles * rows :, :].astype(jnp.int32).astype(jnp.float32)
    return jnp.exp2(raw) * (1.0 / FULL)


def payload_of(tiles, rows, slices):
    return jax.ShapeDtypeStruct((tiles * rows + round_up(tiles, 16), slices), jnp.int16)


def split(value, size):
    if size & (size - 1) == 0:
        return lax.shift_right_logical(value, size.bit_length() - 1), value & (size - 1)
    return lax.div(value, size), lax.rem(value, size)


def cell_of(ray, zi, xi, tiles, outers, inners):
    owner, tile = split(ray, tiles)
    inner, outer = split(owner, outers)
    return ((outer ^ xi) * inners + (inner ^ zi)) * tiles + tile


def place_slots(pos, ray_ref, cell_ref, sizes):
    outers, inners, tiles = sizes

    @pl.loop(0, ray_ref.shape[0], unroll=4)
    def _(s):
        cell_ref[s] = cell_of(ray_ref[s], pos[0], pos[1], tiles, outers, inners)


def list_slots(cell_ref, slots, ranges, slot_list):
    def look(s, count):
        slot_list[count] = s
        cell = cell_ref[s]
        hit = jnp.bool_(False)
        for low, high in ranges:
            hit = hit | ((cell >= low) & (cell < high))
        return count + hit.astype(jnp.int32)

    return lax.fori_loop(slots[0], slots[1], look, jnp.int32(0), unroll=4)


def project(count, together, low, spare, slot_list, cell_ref, pixel_ref, projector_ref, volume_ref, total):
    per_slot = projector_ref.shape[1]

    @pl.loop(0, (count + together - 1) // together)
    def _(i):
        parts, places = [], []
        for u in range(together):
            at = i * together + u
            real = at < count
            s = jnp.where(real, slot_list[at], 0)
            left = jnp.concatenate([projector_ref[s, g] for g in range(per_slot)], axis=1)
            right = jnp.concatenate([volume_ref[pixel_ref[g, s]] for g in range(per_slot)], axis=0)
            parts.append(jnp.dot(left, right, preferred_element_type=jnp.float32))
            places.append(jnp.where(real, cell_ref[s] - low, spare))
        for place, part in zip(places, parts):
            total[place] += part


def joined(tile, t, arrived):
    rows = tile.shape[0]
    for ref, first, count, factor in arrived:
        if first <= t < first + count:
            tile = tile + unpack(ref, factor, t - first, rows)
    return tile


def with_scales(refs, spans, rows):
    return [(ref, first, count, scales(ref, count, rows)) for ref, (first, count) in zip(refs, spans)]


def send_out(total, base, tiles, arrived, send, levels):
    rows = total.shape[1]
    levels[...] = jnp.zeros_like(levels)
    for t in range(tiles):
        pack(joined(total[base + t], t, arrived), send, levels, t)
    send[tiles * rows :, :] = levels[...].astype(jnp.int32).astype(jnp.int16)


def first_kernel(
    sizes, low, ray_hbm, pixel_hbm, projector_hbm, volume_hbm,
    send, projector_ref, volume_ref, out_ref, ray_ref, table_ref, slot_list, total, levels, sems,
):
    slots = ray_ref.shape[0]
    tiles = sizes[2]
    blocks = sems.shape[0] - 4
    cell_ref, pixel_ref = table_ref.at[0], table_ref.at[pl.ds(8, pixel_hbm.shape[0])]
    block = slots // blocks
    pairs = [(ray_hbm, ray_ref), (pixel_hbm, pixel_ref), (volume_hbm, volume_ref)]
    for b in range(blocks):
        span = pl.ds(b * block, block)
        pairs.append((projector_hbm.at[span], projector_ref.at[span]))
    copies = [
        pltpu.make_async_copy(source, target, sems.at[i]) for i, (source, target) in enumerate(pairs)
    ]
    for copy in copies:
        copy.start()
    total[...] = jnp.zeros_like(total)
    copies[0].wait()
    place_slots((lax.axis_index("inner"), lax.axis_index("outer")), ray_ref, cell_ref, sizes)
    copies[1].wait()
    table_copy = pltpu.make_async_copy(table_ref, out_ref, sems.at[3 + blocks])
    table_copy.start()
    copies[2].wait()
    for b in range(blocks):
        count = list_slots(cell_ref, (b * block, b * block + block), [(low, low + tiles)], slot_list)
        copies[3 + b].wait()
        project(
            count, 2, low, tiles, slot_list, cell_ref, pixel_ref, projector_ref, volume_ref, total
        )
    send_out(total, 0, tiles, [], send, levels)
    table_copy.wait()


def hold(value):
    return pltpu.with_memory_space_constraint(value, pltpu.HBM)


def first_send(slot_ray, pixel, projector, volume, sizes, low):
    slots, per_slot, rows, cols = projector.shape
    tiles = sizes[2]
    table = (8 + per_slot, slots)
    slices = volume.shape[2]
    return pl.pallas_call(
        functools.partial(first_kernel, sizes, low),
        in_specs=[HBM, HBM, HBM, HBM],
        out_specs=[VMEM, VMEM, VMEM, VMEM],
        out_shape=[
            payload_of(tiles, rows, slices),
            jax.ShapeDtypeStruct(projector.shape, projector.dtype),
            jax.ShapeDtypeStruct(volume.shape, volume.dtype),
            jax.ShapeDtypeStruct(table, jnp.int32),
        ],
        scratch_shapes=[
            pltpu.SMEM(slot_ray.shape, jnp.int32),
            pltpu.SMEM(table, jnp.int32),
            pltpu.SMEM((slots + UNROLL,), jnp.int32),
            pltpu.VMEM((tiles + 1, rows, slices), jnp.float32),
            pltpu.VMEM((round_up(tiles, 16), slices), jnp.float32),
            pltpu.SemaphoreType.DMA((4 + math.gcd(slots, 4),)),
        ],
        compiler_params=pltpu.CompilerParams(vmem_limit_bytes=48 * 2**20),
        cost_estimate=QUICK,
    )(hold(slot_ray), hold(pixel), hold(projector), hold(volume))


def further_kernel(tiles, sent, ranges, table_ref, projector_ref, volume_ref, after, *rest):
    sends = rest[: len(sent)]
    *own_ref, slot_list, total, levels = rest[len(sent) :]
    slots, per_slot = projector_ref.shape[:2]
    cell_ref, pixel_ref = table_ref.at[0], table_ref.at[pl.ds(8, per_slot)]
    for send, low in zip(sends, sent):
        total[...] = jnp.zeros_like(total)
        count = list_slots(cell_ref, (0, slots), [(low, low + tiles)], slot_list)
        project(
            count, 2, low, tiles, slot_list, cell_ref, pixel_ref, projector_ref, volume_ref, total
        )
        send_out(total, 0, tiles, [], send, levels)
    base = 0
    for ref in own_ref:
        ref[...] = jnp.zeros_like(ref)
        for low, high in ranges:
            count = list_slots(cell_ref, (0, slots), [(low, high)], slot_list)
            project(
                count, UNROLL, low - base, ref.shape[0] - 1, slot_list, cell_ref, pixel_ref,
                projector_ref, volume_ref, ref,
            )
            base += high - low


def further_sums(table, projector, volume, tiles, sent, ranges, after):
    slots, per_slot, rows, cols = projector.shape
    slices = volume.shape[2]
    kept = sum(high - low for low, high in ranges)
    out_shape = [payload_of(tiles, rows, slices)] * len(sent)
    if kept:
        out_shape.append(jax.ShapeDtypeStruct((kept + 1, rows, slices), jnp.float32))
    return pl.pallas_call(
        functools.partial(further_kernel, tiles, sent, ranges),
        in_specs=[SMEM, VMEM, VMEM, ANY],
        out_specs=[VMEM] * len(out_shape),
        out_shape=out_shape,
        scratch_shapes=[
            pltpu.SMEM((slots + UNROLL,), jnp.int32),
            pltpu.VMEM((tiles + 1, rows, slices), jnp.float32),
            pltpu.VMEM((round_up(tiles, 16), slices), jnp.float32),
        ],
        compiler_params=PARAMS,
        cost_estimate=QUICK,
    )(table, projector, volume, after)


def combine_kernel(low, part, spans, own_ref, after, *rest):
    refs, (out_ref, levels) = rest[: len(spans)], rest[len(spans) :]
    send_out(own_ref, low, part, with_scales(refs, spans, own_ref.shape[1]), out_ref, levels)


def combine(own, low, part, arrived, after):
    _, rows, slices = own.shape
    return pl.pallas_call(
        functools.partial(combine_kernel, low, part, [(0, part)] * len(arrived)),
        in_specs=[VMEM, ANY] + [VMEM] * len(arrived),
        out_specs=VMEM,
        out_shape=payload_of(part, rows, slices),
        scratch_shapes=[pltpu.VMEM((round_up(part, 16), slices), jnp.float32)],
        compiler_params=PARAMS,
        cost_estimate=QUICK,
    )(own, after, *arrived)


def gather_kernel(spans, own_ref, *rest):
    refs, out_ref = rest[: len(spans)], rest[len(spans)]
    arrived = with_scales(refs, spans, own_ref.shape[1])
    for t in range(out_ref.shape[0]):
        out_ref[t] = joined(own_ref[t], t, arrived)


def gather(own, tiles, spans, arrived):
    return pl.pallas_call(
        functools.partial(gather_kernel, spans),
        in_specs=[VMEM] * (1 + len(arrived)),
        out_specs=VMEM,
        out_shape=jax.ShapeDtypeStruct((tiles,) + own.shape[1:], jnp.float32),
        compiler_params=PARAMS,
        cost_estimate=QUICK,
    )(own, *arrived)


def weight_kernel(table_ref, index_ref, after, out_ref):
    looked = jnp.zeros(index_ref.shape, jnp.float32)
    for c in range(table_ref.shape[0]):
        looked = jnp.where(index_ref[...] == c, table_ref[c], looked)
    for t in range(index_ref.shape[0]):
        wide = jnp.broadcast_to(looked[t : t + 1, :], (out_ref.shape[2], out_ref.shape[1]))
        out_ref[t] = wide.T.astype(jnp.bfloat16)


def ray_weights(table, index, slices, after):
    tiles, rows = index.shape
    return pl.pallas_call(
        weight_kernel,
        in_specs=[SMEM, VMEM, ANY],
        out_specs=VMEM,
        out_shape=jax.ShapeDtypeStruct((tiles, rows, slices), jnp.bfloat16),
        compiler_params=PARAMS,
        cost_estimate=QUICK,
    )(table.astype(jnp.float32), index, after)


def residual_kernel(spans, sum_ref, sinogram_ref, weight_ref, *rest):
    refs, out_refs = rest[: len(spans)], rest[len(spans) :]
    arrived = with_scales(refs, spans, sum_ref.shape[1])
    part = out_refs[0].shape[0]
    for t in range(sum_ref.shape[0]):
        gap = sinogram_ref[t].astype(jnp.float32) - joined(sum_ref[t], t, arrived)
        out_refs[t // part][t % part] = (weight_ref[t].astype(jnp.float32) * gap).astype(
            jnp.bfloat16
        )


def residual_of(sums, sinogram, weights, part, spans, arrived):
    tiles, rows, slices = sinogram.shape
    return pl.pallas_call(
        functools.partial(residual_kernel, spans),
        in_specs=[VMEM] * (3 + len(arrived)),
        out_specs=[VMEM] * (tiles // part),
        out_shape=[jax.ShapeDtypeStruct((part, rows, slices), jnp.bfloat16)] * (tiles // part),
        compiler_params=PARAMS,
        cost_estimate=QUICK,
    )(sums, sinogram, weights, *arrived)


def column_kernel(table_ref, projector_ref, after, out_ref):
    slots, per_slot, rows, cols = projector_ref.shape
    out_ref[...] = jnp.zeros_like(out_ref)

    @pl.loop(0, slots)
    def _(s):
        for g in range(per_slot):
            column = jnp.sum(projector_ref[s, g].astype(jnp.float32), axis=0, keepdims=True)
            out_ref[table_ref[8 + g, s]] += column


def column_sums(table, projector, patch_tiles, after):
    slots, per_slot, rows, cols = projector.shape
    return pl.pallas_call(
        column_kernel,
        in_specs=[SMEM, VMEM, ANY],
        out_specs=VMEM,
        out_shape=jax.ShapeDtypeStruct((patch_tiles, 1, cols), jnp.float32),
        compiler_params=PARAMS,
        cost_estimate=QUICK,
    )(table, projector, after)


def spread_kernel(lows, begin, finish, table_ref, projector_ref, *rest):
    rest = list(rest)
    before = None if begin else rest.pop(0)
    volume_ref, column_ref = (rest.pop(0), rest.pop(0)) if finish else (None, None)
    chunks, (out_ref, slot_list, held), total = rest[: len(lows)], rest[len(lows) : len(lows) + 3], rest[-1]
    slots, per_slot, rows, cols = projector_ref.shape
    part = chunks[0].shape[0]
    patch_tiles = total.shape[0] - 1
    for low, chunk in zip(lows, chunks):
        held[low : low + part] = chunk[...]
    if begin:
        total[...] = jnp.zeros_like(total)
    else:
        total[...] = before[...]
    count = list_slots(table_ref.at[0], (0, slots), [(low, low + part) for low in lows], slot_list)

    @pl.loop(0, (count + UNROLL - 1) // UNROLL)
    def _(i):
        parts, places = [], []
        for u in range(UNROLL):
            real = i * UNROLL + u < count
            s = jnp.where(real, slot_list[i * UNROLL + u], slot_list[0])
            right = jnp.concatenate([projector_ref[s, g] for g in range(per_slot)], axis=1)
            parts.append(
                lax.dot_general(
                    held[table_ref[0, s]], right, (((0,), (0,)), ((), ())), preferred_element_type=jnp.float32
                )
            )
            places.append([jnp.where(real, table_ref[8 + g, s], patch_tiles) for g in range(per_slot)])
        for part, place in zip(parts, places):
            for g in range(per_slot):
                total[place[g]] += part[:, g * cols : (g + 1) * cols]

    if finish:
        for q in range(patch_tiles):
            out_ref[q] = volume_ref[q].astype(jnp.float32) + (total[q] / column_ref[q]).T


def spread(table, projector, all_cells, lows, chunks, patch_tiles, before, last=()):
    slots, per_slot, rows, cols = projector.shape
    slices = chunks[0].shape[2]
    begin, finish = before is None, bool(last)
    more = ([] if begin else [before]) + list(last) + chunks
    shape = (patch_tiles + 1, slices, cols)
    scratch = [
        pltpu.SMEM((slots + UNROLL,), jnp.int32),
        pltpu.VMEM((all_cells, rows, slices), jnp.bfloat16),
    ]
    kernel = functools.partial(spread_kernel, lows, begin, finish)
    if not finish:
        inner = kernel
        kernel = lambda *refs: inner(*refs, refs[-3])
    return pl.pallas_call(
        kernel,
        in_specs=[SMEM] + [VMEM] * (1 + len(more)),
        out_specs=VMEM,
        out_shape=jax.ShapeDtypeStruct((patch_tiles, cols, slices) if finish else shape, jnp.float32),
        scratch_shapes=scratch + ([pltpu.VMEM(shape, jnp.float32)] if finish else []),
        compiler_params=PARAMS,
        cost_estimate=QUICK,
    )(table, projector, *more)


def gate(value, *after):
    return pl.pallas_call(
        lambda *refs: None,
        in_specs=[VMEM] * (1 + len(after)),
        out_specs=VMEM,
        out_shape=jax.ShapeDtypeStruct(value.shape, value.dtype),
        input_output_aliases={0: 0},
        compiler_params=PARAMS,
        cost_estimate=QUICK,
    )(value, *after)


def dense_plan(volume, projector, slot_ray, slot_pixel, sinogram, weight_index, weight_table):
    inners = lax.axis_size("inner")
    outers = lax.axis_size("outer")
    tiles = sinogram.shape[0]
    patch_tiles, _, slices = volume.shape
    sizes = (outers, inners, tiles)
    pixel = slot_pixel.T

    turns = sorted(range(inners), key=lambda k: (bin(k).count("1"), k))
    far = [k for k in reversed(turns) if k > 1]
    others = range(1, outers)
    low = lambda j, k: (j * inners + k) * tiles
    arrived = {(j, k): [] for j in range(outers) for k in range(inners)}
    first, *sent = [(j, k) for k in far[:1] for j in others]
    near = [(j, 1) for j in others]
    sent += [(j, k) for k in far[1:] for j in others]
    payload, projector, volume, table = first_send(
        slot_ray, pixel, projector, volume, sizes, low(*first)
    )
    kept = [(0, inners * tiles)] + [(low(j, 0), low(j, 0) + tiles) for j in others]
    sends = {first: payload}
    payloads = further_sums(
        table, projector, volume, tiles, [low(*piece) for piece in near], [], payload
    )
    sends.update(zip(near, payloads))
    kept = [(low(0, 2), low(1, 0)), (0, low(0, 2)), (low(1, 0), low(1, 0) + tiles)]
    *payloads, own = further_sums(
        table, projector, volume, tiles, [low(*piece) for piece in sent], kept[:1], payloads[-1]
    )
    sends.update(zip(sent, payloads))
    for k in far[:1]:
        for j in others:
            arrived[0, k].append(swap(sends[j, k], "outer", j))
    for j in others:
        arrived[j, 0].append(swap(sends[j, 1], "inner", 1))
    after = own
    for i, k in enumerate(far):
        bit = k & -k
        after = combine(own, low(0, k) - low(0, 2), tiles, arrived[0, k], after)
        arrived[0, k ^ bit].append(swap(after, "inner", bit))
        if i == 0:
            (near_own,) = further_sums(table, projector, volume, tiles, [], kept[1:], after)
            for l in far[1:]:
                for j in others:
                    payload = gate(sends[j, l], after) if LATER else sends[j, l]
                    arrived[0, l].append(swap(payload, "outer", j))
            for j in others:
                after = combine(near_own, 2 * tiles, tiles, arrived[j, 0], after)
                arrived[0, 0].append(swap(after, "outer", j))
    after = combine(near_own, tiles, tiles, [], after)
    arrived[0, 0].append(swap(after, "inner", 1))
    columns = column_sums(table, projector, patch_tiles, after)
    weights = ray_weights(weight_table, weight_index, slices, columns)
    longest = arrived[0, 0][-2:-1]
    rest = arrived[0, 0][:-2] + arrived[0, 0][-1:]
    span = (0, tiles)
    sums = gather(near_own, tiles, [span] * len(longest), longest)
    residual = residual_of(sums, sinogram, weights, tiles, [span] * len(rest), rest)[0]

    chunks = {(0, 0): residual}
    total = None

    def add(pieces, last=()):
        nonlocal total
        total = spread(
            table, projector, outers * inners * tiles, [low(*piece) for piece in pieces],
            [chunks[piece] for piece in pieces], patch_tiles, total, last,
        )

    bit = inners // 2
    while bit:
        chunks[0, bit] = swap(residual, "inner", bit)
        bit //= 2
    for j in others:
        chunks[j, 0] = swap(residual, "outer", j)
    done = {(0, 0), (0, 1)} | {(j, 0) for j in others}
    for i, k in enumerate(turns[2:]):
        if i == 0 and EARLY:
            for j in others:
                chunks[j, 1] = swap(chunks[j, 0], "inner", 1)
            chunks[0, k] = gate(chunks[0, k], chunks[0, 1], *[chunks[j, 0] for j in others])
        if k == turns[-1]:
            done |= {(0, l) for l in turns[:-1]}
            add(sorted(done))
            chunks[0, k] = gate(chunks[0, k], total)
        bit = (k & -k) // 2
        while bit:
            chunks[0, k ^ bit] = swap(chunks[0, k], "inner", bit)
            bit //= 2
        for j in others:
            chunks[j, k] = swap(chunks[0, k], "outer", j)
    if not EARLY:
        for j in others:
            chunks[j, 1] = swap(gate(chunks[j, 0], chunks[0, turns[-1]]), "inner", 1)
    ends = [(j, turns[-1]) for j in others] + ([] if EARLY else [(j, 1) for j in others])
    add([piece for piece in chunks if piece not in ends and piece not in done])
    add(ends, (volume, columns))
    return total


def slot_plan(volume, projector, slot_ray, slot_pixel, sinogram, weight_index, weight_table):
    inners = lax.axis_size("inner")
    outers = lax.axis_size("outer")
    slot_count = projector.shape[0]
    per_slot = projector.shape[1]
    tile_rows = projector.shape[2]
    tile_cols = projector.shape[3]
    patch_tiles = volume.shape[0]
    slice_count = volume.shape[2]
    owned_rows = sinogram.shape[0]
    band_rows = owned_rows * outers
    capacity = 2 * slot_count // inners
    cell_count = inners * capacity
    target = slot_ray // band_rows
    offset = slot_ray % band_rows
    same_target = target[:, None] == target[None, :]
    earlier = jnp.arange(slot_count)[:, None] > jnp.arange(slot_count)[None, :]
    slot_rank = jnp.sum(jnp.logical_and(same_target, earlier), axis=1)
    position = target * capacity + slot_rank
    partial_value = jnp.zeros((slot_count, tile_rows, slice_count), jnp.float32)
    for column in range(per_slot):
        pixels = volume[slot_pixel[:, column]]
        partial_value = partial_value + jnp.einsum(
            "srp,spc->src", projector[:, column], pixels, preferred_element_type=jnp.float32
        )
    outgoing = (
        jnp.zeros((cell_count, tile_rows, slice_count), jnp.float32).at[position].set(partial_value)
    )
    labels = jnp.full((cell_count,), -1.0, jnp.float32).at[position].set(offset.astype(jnp.float32))
    arrived, arrived_rows = (
        lax.all_to_all(
            outgoing.reshape(inners, capacity, tile_rows, slice_count),
            "inner",
            split_axis=0,
            concat_axis=0,
            tiled=True,
        ),
        lax.all_to_all(
            labels.reshape(inners, capacity), "inner", split_axis=0, concat_axis=0, tiled=True
        ),
    )
    selector = (
        jnp.arange(band_rows, dtype=jnp.float32)[:, None] == arrived_rows.reshape(1, cell_count)
    ).astype(jnp.float32)
    block_sums = jnp.dot(
        selector,
        arrived.reshape(cell_count, tile_rows * slice_count),
        precision=lax.Precision.HIGHEST,
    ).reshape(band_rows, tile_rows, slice_count)
    classes = weight_table.shape[0]
    lookup = weight_index[:, :, None] == jnp.arange(classes)[None, None, :]
    weights = jnp.sum(
        jnp.where(lookup, weight_table[None, None, :], jnp.zeros((), weight_table.dtype)), axis=2
    )
    own_sums = lax.psum_scatter(block_sums, "outer", scatter_dimension=0, tiled=True)
    own_residual = (
        weights.astype(jnp.float32)[:, :, None] * (sinogram.astype(jnp.float32) - own_sums)
    ).astype(jnp.bfloat16)
    residual = lax.all_gather(own_residual, "outer", axis=0, tiled=True)
    picked = jnp.dot(
        selector.T.astype(jnp.bfloat16),
        residual.reshape(band_rows, tile_rows * slice_count),
        preferred_element_type=jnp.float32,
    ).astype(jnp.bfloat16)
    returned = lax.all_to_all(
        picked.reshape(inners, capacity, tile_rows, slice_count),
        "inner",
        split_axis=0,
        concat_axis=0,
        tiled=True,
    )
    slot_residual = returned.reshape(cell_count, tile_rows, slice_count)[position]
    owners = jnp.arange(patch_tiles)
    backward_sum = jnp.zeros((patch_tiles, tile_cols, slice_count), jnp.float32)
    column_sum = jnp.zeros((patch_tiles, tile_cols), jnp.float32)
    for column in range(per_slot):
        member = (owners[:, None] == slot_pixel[None, :, column]).astype(jnp.float32)
        spread = jnp.einsum(
            "srp,src->spc", projector[:, column], slot_residual, preferred_element_type=jnp.float32
        )
        backward_sum = backward_sum + jnp.einsum(
            "ts,spc->tpc", member, spread, precision=lax.Precision.HIGHEST
        )
        column_sum = column_sum + jnp.dot(
            member,
            jnp.sum(projector[:, column], axis=1, dtype=jnp.float32),
            precision=lax.Precision.HIGHEST,
        )
    return volume.astype(jnp.float32) + backward_sum / column_sum[:, :, None]


def on_device(volume, projector, slot_ray, slot_pixel, sinogram, weight_index, weight_table):
    inners = lax.axis_size("inner")
    outers = lax.axis_size("outer")
    capacity = 2 * slot_ray.shape[0] // inners
    powers = inners & (inners - 1) == 0 and outers & (outers - 1) == 0 and inners > 1 < outers
    plan = dense_plan if powers and sinogram.shape[0] * outers <= capacity else slot_plan
    return plan(volume, projector, slot_ray, slot_pixel, sinogram, weight_index, weight_table)


def solution(mesh):
    in_specs = (
        P(("group", "inner", "outer"), None, "cuts"),
        P(("inner", "outer"), None, None, None),
        P(("inner", "outer")),
        P(("inner", "outer"), None),
        P(("group", "inner", "outer"), None, "cuts"),
        P(("group", "inner", "outer"), None),
        P(),
    )
    out_specs = P(("group", "inner", "outer"), None, "cuts")
    return jax.shard_map(
        on_device, mesh=mesh, in_specs=in_specs, out_specs=out_specs, check_vma=False
    )
```

```python
import functools
import math

import jax
import jax.numpy as jnp
from jax import lax
from jax.experimental import pallas as pl
from jax.experimental.pallas import tpu as pltpu
from jax.sharding import PartitionSpec as P

FULL = 32700.0
UNROLL = 4
LATER = True
EARLY = False
VMEM = pl.BlockSpec(memory_space=pltpu.VMEM)
SMEM = pl.BlockSpec(memory_space=pltpu.SMEM)
HBM = pl.BlockSpec(memory_space=pltpu.HBM)
ANY = pl.BlockSpec(memory_space=pl.ANY)
QUICK = pl.CostEstimate(flops=1, bytes_accessed=1, transcendentals=0)
PARAMS = pltpu.CompilerParams(vmem_limit_bytes=24 * 2**20)


def round_up(value, step):
    return -(-value // step) * step


def swap(value, axis, bits):
    size = lax.axis_size(axis)
    return lax.ppermute(value, axis, [(i, i ^ bits) for i in range(size)])


def pack(tile, out_ref, levels_ref, t):
    rows = tile.shape[0]
    top = jnp.maximum(jnp.max(jnp.abs(tile), axis=0, keepdims=True), 1e-30)
    level = jnp.ceil(jnp.log2(top))
    out_ref[t * rows : (t + 1) * rows, :] = (
        jnp.round(tile * (FULL * jnp.exp2(-level))).astype(jnp.int32).astype(jnp.int16)
    )
    levels_ref[t : t + 1, :] = level


def unpack(ref, scale, t, rows):
    block = ref[t * rows : (t + 1) * rows, :]
    return block.astype(jnp.int32).astype(jnp.float32) * scale[t : t + 1, :]


def scales(ref, tiles, rows):
    raw = ref[tiles * rows :, :].astype(jnp.int32).astype(jnp.float32)
    return jnp.exp2(raw) * (1.0 / FULL)


def payload_of(tiles, rows, slices):
    return jax.ShapeDtypeStruct((tiles * rows + round_up(tiles, 16), slices), jnp.int16)


def split(value, size):
    if size & (size - 1) == 0:
        return lax.shift_right_logical(value, size.bit_length() - 1), value & (size - 1)
    return lax.div(value, size), lax.rem(value, size)


def cell_of(ray, zi, xi, tiles, outers, inners):
    owner, tile = split(ray, tiles)
    inner, outer = split(owner, outers)
    return ((outer ^ xi) * inners + (inner ^ zi)) * tiles + tile


def place_slots(pos, ray_ref, cell_ref, sizes):
    outers, inners, tiles = sizes

    @pl.loop(0, ray_ref.shape[0], unroll=4)
    def _(s):
        cell_ref[s] = cell_of(ray_ref[s], pos[0], pos[1], tiles, outers, inners)


def list_slots(cell_ref, slots, ranges, slot_list):
    def look(s, count):
        slot_list[count] = s
        cell = cell_ref[s]
        hit = jnp.bool_(False)
        for low, high in ranges:
            hit = hit | ((cell >= low) & (cell < high))
        return count + hit.astype(jnp.int32)

    return lax.fori_loop(slots[0], slots[1], look, jnp.int32(0), unroll=4)


def project(count, together, low, spare, slot_list, cell_ref, pixel_ref, projector_ref, volume_ref, total):
    per_slot = projector_ref.shape[1]

    @pl.loop(0, (count + together - 1) // together)
    def _(i):
        parts, places = [], []
        for u in range(together):
            at = i * together + u
            real = at < count
            s = jnp.where(real, slot_list[at], 0)
            left = jnp.concatenate([projector_ref[s, g] for g in range(per_slot)], axis=1)
            right = jnp.concatenate([volume_ref[pixel_ref[g, s]] for g in range(per_slot)], axis=0)
            parts.append(jnp.dot(left, right, preferred_element_type=jnp.float32))
            places.append(jnp.where(real, cell_ref[s] - low, spare))
        for place, part in zip(places, parts):
            total[place] += part


def joined(tile, t, arrived):
    rows = tile.shape[0]
    for ref, first, count, factor in arrived:
        if first <= t < first + count:
            tile = tile + unpack(ref, factor, t - first, rows)
    return tile


def with_scales(refs, spans, rows):
    return [(ref, first, count, scales(ref, count, rows)) for ref, (first, count) in zip(refs, spans)]


def send_out(total, base, tiles, arrived, send, levels):
    rows = total.shape[1]
    levels[...] = jnp.zeros_like(levels)
    for t in range(tiles):
        pack(joined(total[base + t], t, arrived), send, levels, t)
    send[tiles * rows :, :] = levels[...].astype(jnp.int32).astype(jnp.int16)


def first_kernel(
    sizes, low, ray_hbm, pixel_hbm, projector_hbm, volume_hbm,
    send, projector_ref, volume_ref, out_ref, ray_ref, table_ref, slot_list, total, levels, sems,
):
    slots = ray_ref.shape[0]
    tiles = sizes[2]
    blocks = sems.shape[0] - 4
    cell_ref, pixel_ref = table_ref.at[0], table_ref.at[pl.ds(8, pixel_hbm.shape[0])]
    block = slots // blocks
    pairs = [(ray_hbm, ray_ref), (pixel_hbm, pixel_ref), (volume_hbm, volume_ref)]
    for b in range(blocks):
        span = pl.ds(b * block, block)
        pairs.append((projector_hbm.at[span], projector_ref.at[span]))
    copies = [
        pltpu.make_async_copy(source, target, sems.at[i]) for i, (source, target) in enumerate(pairs)
    ]
    for copy in copies:
        copy.start()
    total[...] = jnp.zeros_like(total)
    copies[0].wait()
    place_slots((lax.axis_index("inner"), lax.axis_index("outer")), ray_ref, cell_ref, sizes)
    copies[1].wait()
    table_copy = pltpu.make_async_copy(table_ref, out_ref, sems.at[3 + blocks])
    table_copy.start()
    copies[2].wait()
    for b in range(blocks):
        count = list_slots(cell_ref, (b * block, b * block + block), [(low, low + tiles)], slot_list)
        copies[3 + b].wait()
        project(
            count, 2, low, tiles, slot_list, cell_ref, pixel_ref, projector_ref, volume_ref, total
        )
    send_out(total, 0, tiles, [], send, levels)
    table_copy.wait()


def hold(value):
    return pltpu.with_memory_space_constraint(value, pltpu.HBM)


def first_send(slot_ray, pixel, projector, volume, sizes, low):
    slots, per_slot, rows, cols = projector.shape
    tiles = sizes[2]
    table = (8 + per_slot, slots)
    slices = volume.shape[2]
    return pl.pallas_call(
        functools.partial(first_kernel, sizes, low),
        in_specs=[HBM, HBM, HBM, HBM],
        out_specs=[VMEM, VMEM, VMEM, VMEM],
        out_shape=[
            payload_of(tiles, rows, slices),
            jax.ShapeDtypeStruct(projector.shape, projector.dtype),
            jax.ShapeDtypeStruct(volume.shape, volume.dtype),
            jax.ShapeDtypeStruct(table, jnp.int32),
        ],
        scratch_shapes=[
            pltpu.SMEM(slot_ray.shape, jnp.int32),
            pltpu.SMEM(table, jnp.int32),
            pltpu.SMEM((slots + UNROLL,), jnp.int32),
            pltpu.VMEM((tiles + 1, rows, slices), jnp.float32),
            pltpu.VMEM((round_up(tiles, 16), slices), jnp.float32),
            pltpu.SemaphoreType.DMA((4 + math.gcd(slots, 4),)),
        ],
        compiler_params=pltpu.CompilerParams(vmem_limit_bytes=48 * 2**20),
        cost_estimate=QUICK,
    )(hold(slot_ray), hold(pixel), hold(projector), hold(volume))


def further_kernel(tiles, sent, ranges, table_from, projector_ref, volume_ref, after, *rest):
    sends = rest[: len(sent)]
    *own_ref, table_ref, sem, slot_list, total, levels = rest[len(sent) :]
    copy = pltpu.make_async_copy(table_from, table_ref, sem)
    copy.start()
    for ref in own_ref:
        ref[...] = jnp.zeros_like(ref)
    copy.wait()
    slots, per_slot = projector_ref.shape[:2]
    cell_ref, pixel_ref = table_ref.at[0], table_ref.at[pl.ds(8, per_slot)]
    for send, low in zip(sends, sent):
        total[...] = jnp.zeros_like(total)
        count = list_slots(cell_ref, (0, slots), [(low, low + tiles)], slot_list)
        project(
            count, 2, low, tiles, slot_list, cell_ref, pixel_ref, projector_ref, volume_ref, total
        )
        send_out(total, 0, tiles, [], send, levels)
    base = 0
    for ref in own_ref:
        for low, high in ranges:
            count = list_slots(cell_ref, (0, slots), [(low, high)], slot_list)
            project(
                count, UNROLL, low - base, ref.shape[0] - 1, slot_list, cell_ref, pixel_ref,
                projector_ref, volume_ref, ref,
            )
            base += high - low


def further_sums(table, projector, volume, tiles, sent, ranges, after):
    slots, per_slot, rows, cols = projector.shape
    slices = volume.shape[2]
    kept = sum(high - low for low, high in ranges)
    out_shape = [payload_of(tiles, rows, slices)] * len(sent)
    if kept:
        out_shape.append(jax.ShapeDtypeStruct((kept + 1, rows, slices), jnp.float32))
    return pl.pallas_call(
        functools.partial(further_kernel, tiles, sent, ranges),
        in_specs=[VMEM, VMEM, VMEM, ANY],
        out_specs=[VMEM] * len(out_shape),
        out_shape=out_shape,
        scratch_shapes=[
            pltpu.SMEM(table.shape, jnp.int32),
            pltpu.SemaphoreType.DMA,
            pltpu.SMEM((slots + UNROLL,), jnp.int32),
            pltpu.VMEM((tiles + 1, rows, slices), jnp.float32),
            pltpu.VMEM((round_up(tiles, 16), slices), jnp.float32),
        ],
        compiler_params=PARAMS,
        cost_estimate=QUICK,
    )(table, projector, volume, after)


def combine_kernel(low, part, spans, own_ref, after, *rest):
    refs, (out_ref, levels) = rest[: len(spans)], rest[len(spans) :]
    send_out(own_ref, low, part, with_scales(refs, spans, own_ref.shape[1]), out_ref, levels)


def combine(own, low, part, arrived, after):
    _, rows, slices = own.shape
    return pl.pallas_call(
        functools.partial(combine_kernel, low, part, [(0, part)] * len(arrived)),
        in_specs=[VMEM, ANY] + [VMEM] * len(arrived),
        out_specs=VMEM,
        out_shape=payload_of(part, rows, slices),
        scratch_shapes=[pltpu.VMEM((round_up(part, 16), slices), jnp.float32)],
        compiler_params=PARAMS,
        cost_estimate=QUICK,
    )(own, after, *arrived)


def gather_kernel(spans, own_ref, *rest):
    refs, out_ref = rest[: len(spans)], rest[len(spans)]
    arrived = with_scales(refs, spans, own_ref.shape[1])
    for t in range(out_ref.shape[0]):
        out_ref[t] = joined(own_ref[t], t, arrived)


def gather(own, tiles, spans, arrived):
    return pl.pallas_call(
        functools.partial(gather_kernel, spans),
        in_specs=[VMEM] * (1 + len(arrived)),
        out_specs=VMEM,
        out_shape=jax.ShapeDtypeStruct((tiles,) + own.shape[1:], jnp.float32),
        compiler_params=PARAMS,
        cost_estimate=QUICK,
    )(own, *arrived)


def weight_kernel(table_ref, index_ref, after, out_ref):
    looked = jnp.zeros(index_ref.shape, jnp.float32)
    for c in range(table_ref.shape[0]):
        looked = jnp.where(index_ref[...] == c, table_ref[c], looked)
    for t in range(index_ref.shape[0]):
        wide = jnp.broadcast_to(looked[t : t + 1, :], (out_ref.shape[2], out_ref.shape[1]))
        out_ref[t] = wide.T.astype(jnp.bfloat16)


def ray_weights(table, index, slices, after):
    tiles, rows = index.shape
    return pl.pallas_call(
        weight_kernel,
        in_specs=[SMEM, VMEM, ANY],
        out_specs=VMEM,
        out_shape=jax.ShapeDtypeStruct((tiles, rows, slices), jnp.bfloat16),
        compiler_params=PARAMS,
        cost_estimate=QUICK,
    )(table.astype(jnp.float32), index, after)


def residual_kernel(spans, sum_ref, sinogram_ref, weight_ref, *rest):
    refs, out_refs = rest[: len(spans)], rest[len(spans) :]
    arrived = with_scales(refs, spans, sum_ref.shape[1])
    part = out_refs[0].shape[0]
    for t in range(sum_ref.shape[0]):
        gap = sinogram_ref[t].astype(jnp.float32) - joined(sum_ref[t], t, arrived)
        out_refs[t // part][t % part] = (weight_ref[t].astype(jnp.float32) * gap).astype(
            jnp.bfloat16
        )


def residual_of(sums, sinogram, weights, part, spans, arrived):
    tiles, rows, slices = sinogram.shape
    return pl.pallas_call(
        functools.partial(residual_kernel, spans),
        in_specs=[VMEM] * (3 + len(arrived)),
        out_specs=[VMEM] * (tiles // part),
        out_shape=[jax.ShapeDtypeStruct((part, rows, slices), jnp.bfloat16)] * (tiles // part),
        compiler_params=PARAMS,
        cost_estimate=QUICK,
    )(sums, sinogram, weights, *arrived)


def column_kernel(table_ref, projector_ref, after, out_ref):
    slots, per_slot, rows, cols = projector_ref.shape
    out_ref[...] = jnp.zeros_like(out_ref)

    @pl.loop(0, slots)
    def _(s):
        for g in range(per_slot):
            column = jnp.sum(projector_ref[s, g].astype(jnp.float32), axis=0, keepdims=True)
            out_ref[table_ref[8 + g, s]] += column


def column_sums(table, projector, patch_tiles, after):
    slots, per_slot, rows, cols = projector.shape
    return pl.pallas_call(
        column_kernel,
        in_specs=[SMEM, VMEM, ANY],
        out_specs=VMEM,
        out_shape=jax.ShapeDtypeStruct((patch_tiles, 1, cols), jnp.float32),
        compiler_params=PARAMS,
        cost_estimate=QUICK,
    )(table, projector, after)


def spread_kernel(lows, begin, finish, table_from, projector_ref, *rest):
    rest = list(rest)
    before = None if begin else rest.pop(0)
    volume_ref, column_ref = (rest.pop(0), rest.pop(0)) if finish else (None, None)
    chunks, (out_ref, table_ref, sem, slot_list, held) = rest[: len(lows)], rest[len(lows) : len(lows) + 5]
    total = rest[-1]
    copy = pltpu.make_async_copy(table_from, table_ref, sem)
    copy.start()
    slots, per_slot, rows, cols = projector_ref.shape
    part = chunks[0].shape[0]
    patch_tiles = total.shape[0] - 1
    for low, chunk in zip(lows, chunks):
        held[low : low + part] = chunk[...]
    if begin:
        total[...] = jnp.zeros_like(total)
    else:
        total[...] = before[...]
    copy.wait()
    count = list_slots(table_ref.at[0], (0, slots), [(low, low + part) for low in lows], slot_list)

    @pl.loop(0, (count + UNROLL - 1) // UNROLL)
    def _(i):
        parts, places = [], []
        for u in range(UNROLL):
            real = i * UNROLL + u < count
            s = jnp.where(real, slot_list[i * UNROLL + u], slot_list[0])
            right = jnp.concatenate([projector_ref[s, g] for g in range(per_slot)], axis=1)
            parts.append(
                lax.dot_general(
                    held[table_ref[0, s]], right, (((0,), (0,)), ((), ())), preferred_element_type=jnp.float32
                )
            )
            places.append([jnp.where(real, table_ref[8 + g, s], patch_tiles) for g in range(per_slot)])
        for part, place in zip(parts, places):
            for g in range(per_slot):
                total[place[g]] += part[:, g * cols : (g + 1) * cols]

    if finish:
        for q in range(patch_tiles):
            out_ref[q] = volume_ref[q].astype(jnp.float32) + (total[q] / column_ref[q]).T


def spread(table, projector, all_cells, lows, chunks, patch_tiles, before, last=()):
    slots, per_slot, rows, cols = projector.shape
    slices = chunks[0].shape[2]
    begin, finish = before is None, bool(last)
    more = ([] if begin else [before]) + list(last) + chunks
    shape = (patch_tiles + 1, slices, cols)
    scratch = [
        pltpu.SMEM(table.shape, jnp.int32),
        pltpu.SemaphoreType.DMA,
        pltpu.SMEM((slots + UNROLL,), jnp.int32),
        pltpu.VMEM((all_cells, rows, slices), jnp.bfloat16),
    ]
    kernel = functools.partial(spread_kernel, lows, begin, finish)
    if not finish:
        inner = kernel
        kernel = lambda *refs: inner(*refs, refs[-5])
    return pl.pallas_call(
        kernel,
        in_specs=[VMEM] * (2 + len(more)),
        out_specs=VMEM,
        out_shape=jax.ShapeDtypeStruct((patch_tiles, cols, slices) if finish else shape, jnp.float32),
        scratch_shapes=scratch + ([pltpu.VMEM(shape, jnp.float32)] if finish else []),
        compiler_params=PARAMS,
        cost_estimate=QUICK,
    )(table, projector, *more)


def gate(value, *after):
    return pl.pallas_call(
        lambda *refs: None,
        in_specs=[VMEM] * (1 + len(after)),
        out_specs=VMEM,
        out_shape=jax.ShapeDtypeStruct(value.shape, value.dtype),
        input_output_aliases={0: 0},
        compiler_params=PARAMS,
        cost_estimate=QUICK,
    )(value, *after)


def dense_plan(volume, projector, slot_ray, slot_pixel, sinogram, weight_index, weight_table):
    inners = lax.axis_size("inner")
    outers = lax.axis_size("outer")
    tiles = sinogram.shape[0]
    patch_tiles, _, slices = volume.shape
    sizes = (outers, inners, tiles)
    pixel = slot_pixel.T

    turns = sorted(range(inners), key=lambda k: (bin(k).count("1"), k))
    far = [k for k in reversed(turns) if k > 1]
    others = range(1, outers)
    low = lambda j, k: (j * inners + k) * tiles
    arrived = {(j, k): [] for j in range(outers) for k in range(inners)}
    first, *sent = [(j, k) for k in far[:1] for j in others]
    near = [(j, 1) for j in others]
    sent += [(j, k) for k in far[1:] for j in others]
    payload, projector, volume, table = first_send(
        slot_ray, pixel, projector, volume, sizes, low(*first)
    )
    kept = [(0, inners * tiles)] + [(low(j, 0), low(j, 0) + tiles) for j in others]
    sends = {first: payload}
    payloads = further_sums(
        table, projector, volume, tiles, [low(*piece) for piece in near], [], payload
    )
    sends.update(zip(near, payloads))
    kept = [(low(0, 2), low(1, 0)), (0, low(0, 2)), (low(1, 0), low(1, 0) + tiles)]
    *payloads, own = further_sums(
        table, projector, volume, tiles, [low(*piece) for piece in sent], kept[:1], payloads[-1]
    )
    sends.update(zip(sent, payloads))
    for k in far[:1]:
        for j in others:
            arrived[0, k].append(swap(sends[j, k], "outer", j))
    for j in others:
        arrived[j, 0].append(swap(sends[j, 1], "inner", 1))
    after = own
    for i, k in enumerate(far):
        bit = k & -k
        after = combine(own, low(0, k) - low(0, 2), tiles, arrived[0, k], after)
        arrived[0, k ^ bit].append(swap(after, "inner", bit))
        if i == 0:
            (near_own,) = further_sums(table, projector, volume, tiles, [], kept[1:], after)
            for l in far[1:]:
                for j in others:
                    payload = gate(sends[j, l], after) if LATER else sends[j, l]
                    arrived[0, l].append(swap(payload, "outer", j))
            for j in others:
                after = combine(near_own, 2 * tiles, tiles, arrived[j, 0], after)
                arrived[0, 0].append(swap(after, "outer", j))
    after = combine(near_own, tiles, tiles, [], after)
    arrived[0, 0].append(swap(after, "inner", 1))
    columns = column_sums(table, projector, patch_tiles, after)
    weights = ray_weights(weight_table, weight_index, slices, columns)
    longest = arrived[0, 0][-2:]
    rest = arrived[0, 0][:-2]
    span = (0, tiles)
    sums = gather(near_own, tiles, [span] * len(longest), longest)
    residual = residual_of(sums, sinogram, weights, tiles, [span] * len(rest), rest)[0]

    chunks = {(0, 0): residual}
    total = None

    def add(pieces, last=()):
        nonlocal total
        total = spread(
            table, projector, outers * inners * tiles, [low(*piece) for piece in pieces],
            [chunks[piece] for piece in pieces], patch_tiles, total, last,
        )

    bit = inners // 2
    while bit:
        chunks[0, bit] = swap(residual, "inner", bit)
        bit //= 2
    for j in others:
        chunks[j, 0] = swap(residual, "outer", j)
    done = {(0, 0), (0, 1)} | {(j, 0) for j in others}
    for i, k in enumerate(turns[2:]):
        if i == 0 and EARLY:
            for j in others:
                chunks[j, 1] = swap(chunks[j, 0], "inner", 1)
            chunks[0, k] = gate(chunks[0, k], chunks[0, 1], *[chunks[j, 0] for j in others])
        if k == turns[-1]:
            done |= {(0, l) for l in turns[:-1]}
            add(sorted(done))
            chunks[0, k] = gate(chunks[0, k], total)
        bit = (k & -k) // 2
        while bit:
            chunks[0, k ^ bit] = swap(chunks[0, k], "inner", bit)
            bit //= 2
        for j in others:
            chunks[j, k] = swap(chunks[0, k], "outer", j)
    if not EARLY:
        for j in others:
            chunks[j, 1] = swap(gate(chunks[j, 0], chunks[0, turns[-1]]), "inner", 1)
    ends = [(j, turns[-1]) for j in others] + ([] if EARLY else [(j, 1) for j in others])
    add([piece for piece in chunks if piece not in ends and piece not in done])
    add(ends, (volume, columns))
    return total


def slot_plan(volume, projector, slot_ray, slot_pixel, sinogram, weight_index, weight_table):
    inners = lax.axis_size("inner")
    outers = lax.axis_size("outer")
    slot_count = projector.shape[0]
    per_slot = projector.shape[1]
    tile_rows = projector.shape[2]
    tile_cols = projector.shape[3]
    patch_tiles = volume.shape[0]
    slice_count = volume.shape[2]
    owned_rows = sinogram.shape[0]
    band_rows = owned_rows * outers
    capacity = 2 * slot_count // inners
    cell_count = inners * capacity
    target = slot_ray // band_rows
    offset = slot_ray % band_rows
    same_target = target[:, None] == target[None, :]
    earlier = jnp.arange(slot_count)[:, None] > jnp.arange(slot_count)[None, :]
    slot_rank = jnp.sum(jnp.logical_and(same_target, earlier), axis=1)
    position = target * capacity + slot_rank
    partial_value = jnp.zeros((slot_count, tile_rows, slice_count), jnp.float32)
    for column in range(per_slot):
        pixels = volume[slot_pixel[:, column]]
        partial_value = partial_value + jnp.einsum(
            "srp,spc->src", projector[:, column], pixels, preferred_element_type=jnp.float32
        )
    outgoing = (
        jnp.zeros((cell_count, tile_rows, slice_count), jnp.float32).at[position].set(partial_value)
    )
    labels = jnp.full((cell_count,), -1.0, jnp.float32).at[position].set(offset.astype(jnp.float32))
    arrived, arrived_rows = (
        lax.all_to_all(
            outgoing.reshape(inners, capacity, tile_rows, slice_count),
            "inner",
            split_axis=0,
            concat_axis=0,
            tiled=True,
        ),
        lax.all_to_all(
            labels.reshape(inners, capacity), "inner", split_axis=0, concat_axis=0, tiled=True
        ),
    )
    selector = (
        jnp.arange(band_rows, dtype=jnp.float32)[:, None] == arrived_rows.reshape(1, cell_count)
    ).astype(jnp.float32)
    block_sums = jnp.dot(
        selector,
        arrived.reshape(cell_count, tile_rows * slice_count),
        precision=lax.Precision.HIGHEST,
    ).reshape(band_rows, tile_rows, slice_count)
    classes = weight_table.shape[0]
    lookup = weight_index[:, :, None] == jnp.arange(classes)[None, None, :]
    weights = jnp.sum(
        jnp.where(lookup, weight_table[None, None, :], jnp.zeros((), weight_table.dtype)), axis=2
    )
    own_sums = lax.psum_scatter(block_sums, "outer", scatter_dimension=0, tiled=True)
    own_residual = (
        weights.astype(jnp.float32)[:, :, None] * (sinogram.astype(jnp.float32) - own_sums)
    ).astype(jnp.bfloat16)
    residual = lax.all_gather(own_residual, "outer", axis=0, tiled=True)
    picked = jnp.dot(
        selector.T.astype(jnp.bfloat16),
        residual.reshape(band_rows, tile_rows * slice_count),
        preferred_element_type=jnp.float32,
    ).astype(jnp.bfloat16)
    returned = lax.all_to_all(
        picked.reshape(inners, capacity, tile_rows, slice_count),
        "inner",
        split_axis=0,
        concat_axis=0,
        tiled=True,
    )
    slot_residual = returned.reshape(cell_count, tile_rows, slice_count)[position]
    owners = jnp.arange(patch_tiles)
    backward_sum = jnp.zeros((patch_tiles, tile_cols, slice_count), jnp.float32)
    column_sum = jnp.zeros((patch_tiles, tile_cols), jnp.float32)
    for column in range(per_slot):
        member = (owners[:, None] == slot_pixel[None, :, column]).astype(jnp.float32)
        spread = jnp.einsum(
            "srp,src->spc", projector[:, column], slot_residual, preferred_element_type=jnp.float32
        )
        backward_sum = backward_sum + jnp.einsum(
            "ts,spc->tpc", member, spread, precision=lax.Precision.HIGHEST
        )
        column_sum = column_sum + jnp.dot(
            member,
            jnp.sum(projector[:, column], axis=1, dtype=jnp.float32),
            precision=lax.Precision.HIGHEST,
        )
    return volume.astype(jnp.float32) + backward_sum / column_sum[:, :, None]


def on_device(volume, projector, slot_ray, slot_pixel, sinogram, weight_index, weight_table):
    inners = lax.axis_size("inner")
    outers = lax.axis_size("outer")
    capacity = 2 * slot_ray.shape[0] // inners
    powers = inners & (inners - 1) == 0 and outers & (outers - 1) == 0 and inners > 1 < outers
    plan = dense_plan if powers and sinogram.shape[0] * outers <= capacity else slot_plan
    return plan(volume, projector, slot_ray, slot_pixel, sinogram, weight_index, weight_table)


def solution(mesh):
    in_specs = (
        P(("group", "inner", "outer"), None, "cuts"),
        P(("inner", "outer"), None, None, None),
        P(("inner", "outer")),
        P(("inner", "outer"), None),
        P(("group", "inner", "outer"), None, "cuts"),
        P(("group", "inner", "outer"), None),
        P(),
    )
    out_specs = P(("group", "inner", "outer"), None, "cuts")
    return jax.shard_map(
        on_device, mesh=mesh, in_specs=in_specs, out_specs=out_specs, check_vma=False
    )
```

```python
import functools
import math

import jax
import jax.numpy as jnp
from jax import lax
from jax.experimental import pallas as pl
from jax.experimental.pallas import tpu as pltpu
from jax.sharding import PartitionSpec as P

FULL = 32700.0
UNROLL = 4
LATER = True
VMEM = pl.BlockSpec(memory_space=pltpu.VMEM)
SMEM = pl.BlockSpec(memory_space=pltpu.SMEM)
HBM = pl.BlockSpec(memory_space=pltpu.HBM)
ANY = pl.BlockSpec(memory_space=pl.ANY)


def weighs(weight):
    return pl.CostEstimate(flops=max(int(weight * 1e9), 1), bytes_accessed=1, transcendentals=0)


QUICK = weighs(0)
PARAMS = pltpu.CompilerParams(vmem_limit_bytes=24 * 2**20)


def round_up(value, step):
    return -(-value // step) * step


def swap(value, axis, bits):
    size = lax.axis_size(axis)
    return lax.ppermute(value, axis, [(i, i ^ bits) for i in range(size)])


def pack(tile, out_ref, levels_ref, t):
    rows = tile.shape[0]
    top = jnp.maximum(jnp.max(jnp.abs(tile), axis=0, keepdims=True), 1e-30)
    level = jnp.ceil(jnp.log2(top))
    out_ref[t * rows : (t + 1) * rows, :] = (
        jnp.round(tile * (FULL * jnp.exp2(-level))).astype(jnp.int32).astype(jnp.int16)
    )
    levels_ref[t : t + 1, :] = level


def unpack(ref, scale, t, rows):
    block = ref[t * rows : (t + 1) * rows, :]
    return block.astype(jnp.int32).astype(jnp.float32) * scale[t : t + 1, :]


def scales(ref, tiles, rows):
    raw = ref[tiles * rows :, :].astype(jnp.int32).astype(jnp.float32)
    return jnp.exp2(raw) * (1.0 / FULL)


def payload_of(tiles, rows, slices):
    return jax.ShapeDtypeStruct((tiles * rows + round_up(tiles, 16), slices), jnp.int16)


def split(value, size):
    if size & (size - 1) == 0:
        return lax.shift_right_logical(value, size.bit_length() - 1), value & (size - 1)
    return lax.div(value, size), lax.rem(value, size)


def cell_of(ray, zi, xi, tiles, outers, inners):
    owner, tile = split(ray, tiles)
    inner, outer = split(owner, outers)
    return ((outer ^ xi) * inners + (inner ^ zi)) * tiles + tile


def place_slots(pos, ray_ref, cell_ref, sizes):
    outers, inners, tiles = sizes

    @pl.loop(0, ray_ref.shape[0], unroll=4)
    def _(s):
        cell_ref[s] = cell_of(ray_ref[s], pos[0], pos[1], tiles, outers, inners)


def list_slots(cell_ref, slots, ranges, slot_list):
    def look(s, count):
        slot_list[count] = s
        cell = cell_ref[s]
        hit = jnp.bool_(False)
        for low, high in ranges:
            hit = hit | ((cell >= low) & (cell < high))
        return count + hit.astype(jnp.int32)

    return lax.fori_loop(slots[0], slots[1], look, jnp.int32(0), unroll=4)


def project(count, together, low, spare, slot_list, cell_ref, pixel_ref, projector_ref, volume_ref, total):
    per_slot = projector_ref.shape[1]

    @pl.loop(0, (count + together - 1) // together)
    def _(i):
        parts, places = [], []
        for u in range(together):
            at = i * together + u
            real = at < count
            s = jnp.where(real, slot_list[at], 0)
            left = jnp.concatenate([projector_ref[s, g] for g in range(per_slot)], axis=1)
            right = jnp.concatenate([volume_ref[pixel_ref[g, s]] for g in range(per_slot)], axis=0)
            parts.append(jnp.dot(left, right, preferred_element_type=jnp.float32))
            places.append(jnp.where(real, cell_ref[s] - low, spare))
        for place, part in zip(places, parts):
            total[place] += part


def joined(tile, t, arrived):
    rows = tile.shape[0]
    for ref, first, count, factor in arrived:
        if first <= t < first + count:
            tile = tile + unpack(ref, factor, t - first, rows)
    return tile


def with_scales(refs, spans, rows):
    return [(ref, first, count, scales(ref, count, rows)) for ref, (first, count) in zip(refs, spans)]


def send_out(total, base, tiles, arrived, send, levels):
    rows = total.shape[1]
    levels[...] = jnp.zeros_like(levels)
    for t in range(tiles):
        pack(joined(total[base + t], t, arrived), send, levels, t)
    send[tiles * rows :, :] = levels[...].astype(jnp.int32).astype(jnp.int16)


def first_kernel(
    sizes, low, ray_hbm, pixel_hbm, projector_hbm, volume_hbm,
    send, projector_ref, volume_ref, out_ref, ray_ref, table_ref, slot_list, total, levels, sems,
):
    slots = ray_ref.shape[0]
    tiles = sizes[2]
    blocks = sems.shape[0] - 4
    cell_ref, pixel_ref = table_ref.at[0], table_ref.at[pl.ds(8, pixel_hbm.shape[0])]
    block = slots // blocks
    pairs = [(ray_hbm, ray_ref), (pixel_hbm, pixel_ref), (volume_hbm, volume_ref)]
    for b in range(blocks):
        span = pl.ds(b * block, block)
        pairs.append((projector_hbm.at[span], projector_ref.at[span]))
    copies = [
        pltpu.make_async_copy(source, target, sems.at[i]) for i, (source, target) in enumerate(pairs)
    ]
    for copy in copies:
        copy.start()
    total[...] = jnp.zeros_like(total)
    copies[0].wait()
    place_slots((lax.axis_index("inner"), lax.axis_index("outer")), ray_ref, cell_ref, sizes)
    copies[1].wait()
    table_copy = pltpu.make_async_copy(table_ref, out_ref, sems.at[3 + blocks])
    table_copy.start()
    copies[2].wait()
    for b in range(blocks):
        count = list_slots(cell_ref, (b * block, b * block + block), [(low, low + tiles)], slot_list)
        copies[3 + b].wait()
        project(
            count, 2, low, tiles, slot_list, cell_ref, pixel_ref, projector_ref, volume_ref, total
        )
    send_out(total, 0, tiles, [], send, levels)
    table_copy.wait()


def hold(value):
    return pltpu.with_memory_space_constraint(value, pltpu.HBM)


def first_send(slot_ray, pixel, projector, volume, sizes, low):
    slots, per_slot, rows, cols = projector.shape
    tiles = sizes[2]
    table = (8 + per_slot, slots)
    slices = volume.shape[2]
    return pl.pallas_call(
        functools.partial(first_kernel, sizes, low),
        in_specs=[HBM, HBM, HBM, HBM],
        out_specs=[VMEM, VMEM, VMEM, VMEM],
        out_shape=[
            payload_of(tiles, rows, slices),
            jax.ShapeDtypeStruct(projector.shape, projector.dtype),
            jax.ShapeDtypeStruct(volume.shape, volume.dtype),
            jax.ShapeDtypeStruct(table, jnp.int32),
        ],
        scratch_shapes=[
            pltpu.SMEM(slot_ray.shape, jnp.int32),
            pltpu.SMEM(table, jnp.int32),
            pltpu.SMEM((slots + UNROLL,), jnp.int32),
            pltpu.VMEM((tiles + 1, rows, slices), jnp.float32),
            pltpu.VMEM((round_up(tiles, 16), slices), jnp.float32),
            pltpu.SemaphoreType.DMA((4 + math.gcd(slots, 4),)),
        ],
        compiler_params=pltpu.CompilerParams(vmem_limit_bytes=48 * 2**20),
        cost_estimate=QUICK,
    )(hold(slot_ray), hold(pixel), hold(projector), hold(volume))


def further_kernel(tiles, sent, ranges, table_from, projector_ref, volume_ref, after, *rest):
    sends = rest[: len(sent)]
    *own_ref, table_ref, sem, slot_list, total, levels = rest[len(sent) :]
    copy = pltpu.make_async_copy(table_from, table_ref, sem)
    copy.start()
    for ref in own_ref:
        ref[...] = jnp.zeros_like(ref)
    copy.wait()
    slots, per_slot = projector_ref.shape[:2]
    cell_ref, pixel_ref = table_ref.at[0], table_ref.at[pl.ds(8, per_slot)]
    for send, low in zip(sends, sent):
        total[...] = jnp.zeros_like(total)
        count = list_slots(cell_ref, (0, slots), [(low, low + tiles)], slot_list)
        project(
            count, 2, low, tiles, slot_list, cell_ref, pixel_ref, projector_ref, volume_ref, total
        )
        send_out(total, 0, tiles, [], send, levels)
    base = 0
    for ref in own_ref:
        for low, high in ranges:
            count = list_slots(cell_ref, (0, slots), [(low, high)], slot_list)
            project(
                count, UNROLL, low - base, ref.shape[0] - 1, slot_list, cell_ref, pixel_ref,
                projector_ref, volume_ref, ref,
            )
            base += high - low


def further_sums(table, projector, volume, tiles, sent, ranges, after):
    slots, per_slot, rows, cols = projector.shape
    slices = volume.shape[2]
    kept = sum(high - low for low, high in ranges)
    out_shape = [payload_of(tiles, rows, slices)] * len(sent)
    if kept:
        out_shape.append(jax.ShapeDtypeStruct((kept + 1, rows, slices), jnp.float32))
    return pl.pallas_call(
        functools.partial(further_kernel, tiles, sent, ranges),
        in_specs=[VMEM, VMEM, VMEM, ANY],
        out_specs=[VMEM] * len(out_shape),
        out_shape=out_shape,
        scratch_shapes=[
            pltpu.SMEM(table.shape, jnp.int32),
            pltpu.SemaphoreType.DMA,
            pltpu.SMEM((slots + UNROLL,), jnp.int32),
            pltpu.VMEM((tiles + 1, rows, slices), jnp.float32),
            pltpu.VMEM((round_up(tiles, 16), slices), jnp.float32),
        ],
        compiler_params=PARAMS,
        cost_estimate=QUICK,
    )(table, projector, volume, after)


def combine_kernel(low, part, spans, own_ref, after, *rest):
    refs, (out_ref, levels) = rest[: len(spans)], rest[len(spans) :]
    send_out(own_ref, low, part, with_scales(refs, spans, own_ref.shape[1]), out_ref, levels)


def combine(own, low, part, arrived, after):
    _, rows, slices = own.shape
    return pl.pallas_call(
        functools.partial(combine_kernel, low, part, [(0, part)] * len(arrived)),
        in_specs=[VMEM, ANY] + [VMEM] * len(arrived),
        out_specs=VMEM,
        out_shape=payload_of(part, rows, slices),
        scratch_shapes=[pltpu.VMEM((round_up(part, 16), slices), jnp.float32)],
        compiler_params=PARAMS,
        cost_estimate=QUICK,
    )(own, after, *arrived)


def gather_kernel(spans, own_ref, *rest):
    refs, out_ref = rest[: len(spans)], rest[len(spans)]
    arrived = with_scales(refs, spans, own_ref.shape[1])
    for t in range(out_ref.shape[0]):
        out_ref[t] = joined(own_ref[t], t, arrived)


def gather(own, tiles, spans, arrived):
    return pl.pallas_call(
        functools.partial(gather_kernel, spans),
        in_specs=[VMEM] * (1 + len(arrived)),
        out_specs=VMEM,
        out_shape=jax.ShapeDtypeStruct((tiles,) + own.shape[1:], jnp.float32),
        compiler_params=PARAMS,
        cost_estimate=QUICK,
    )(own, *arrived)


def weight_kernel(table_ref, index_ref, after, out_ref):
    looked = jnp.zeros(index_ref.shape, jnp.float32)
    for c in range(table_ref.shape[0]):
        looked = jnp.where(index_ref[...] == c, table_ref[c], looked)
    for t in range(index_ref.shape[0]):
        wide = jnp.broadcast_to(looked[t : t + 1, :], (out_ref.shape[2], out_ref.shape[1]))
        out_ref[t] = wide.T.astype(jnp.bfloat16)


def ray_weights(table, index, slices, after):
    tiles, rows = index.shape
    return pl.pallas_call(
        weight_kernel,
        in_specs=[SMEM, VMEM, ANY],
        out_specs=VMEM,
        out_shape=jax.ShapeDtypeStruct((tiles, rows, slices), jnp.bfloat16),
        compiler_params=PARAMS,
        cost_estimate=QUICK,
    )(table.astype(jnp.float32), index, after)


def residual_kernel(spans, sum_ref, sinogram_ref, weight_ref, *rest):
    refs, out_refs = rest[: len(spans)], rest[len(spans) :]
    arrived = with_scales(refs, spans, sum_ref.shape[1])
    part = out_refs[0].shape[0]
    for t in range(sum_ref.shape[0]):
        gap = sinogram_ref[t].astype(jnp.float32) - joined(sum_ref[t], t, arrived)
        out_refs[t // part][t % part] = (weight_ref[t].astype(jnp.float32) * gap).astype(
            jnp.bfloat16
        )


def residual_of(sums, sinogram, weights, part, spans, arrived):
    tiles, rows, slices = sinogram.shape
    return pl.pallas_call(
        functools.partial(residual_kernel, spans),
        in_specs=[VMEM] * (3 + len(arrived)),
        out_specs=[VMEM] * (tiles // part),
        out_shape=[jax.ShapeDtypeStruct((part, rows, slices), jnp.bfloat16)] * (tiles // part),
        compiler_params=PARAMS,
        cost_estimate=QUICK,
    )(sums, sinogram, weights, *arrived)


def column_kernel(table_ref, projector_ref, after, out_ref):
    slots, per_slot, rows, cols = projector_ref.shape
    out_ref[...] = jnp.zeros_like(out_ref)

    @pl.loop(0, slots)
    def _(s):
        for g in range(per_slot):
            column = jnp.sum(projector_ref[s, g].astype(jnp.float32), axis=0, keepdims=True)
            out_ref[table_ref[8 + g, s]] += column


def column_sums(table, projector, patch_tiles, after):
    slots, per_slot, rows, cols = projector.shape
    return pl.pallas_call(
        column_kernel,
        in_specs=[SMEM, VMEM, ANY],
        out_specs=VMEM,
        out_shape=jax.ShapeDtypeStruct((patch_tiles, 1, cols), jnp.float32),
        compiler_params=PARAMS,
        cost_estimate=QUICK,
    )(table, projector, after)


def spread_kernel(lows, begin, finish, table_from, projector_ref, *rest):
    rest = list(rest)
    before = None if begin else rest.pop(0)
    volume_ref, column_ref = (rest.pop(0), rest.pop(0)) if finish else (None, None)
    chunks, (out_ref, table_ref, sem, slot_list, held) = rest[: len(lows)], rest[len(lows) : len(lows) + 5]
    total = rest[-1]
    copy = pltpu.make_async_copy(table_from, table_ref, sem)
    copy.start()
    slots, per_slot, rows, cols = projector_ref.shape
    part = chunks[0].shape[0]
    patch_tiles = total.shape[0] - 1
    for low, chunk in zip(lows, chunks):
        held[low : low + part] = chunk[...]
    if begin:
        total[...] = jnp.zeros_like(total)
    else:
        total[...] = before[...]
    copy.wait()
    count = list_slots(table_ref.at[0], (0, slots), [(low, low + part) for low in lows], slot_list)

    @pl.loop(0, (count + UNROLL - 1) // UNROLL)
    def _(i):
        parts, places = [], []
        for u in range(UNROLL):
            real = i * UNROLL + u < count
            s = jnp.where(real, slot_list[i * UNROLL + u], slot_list[0])
            right = jnp.concatenate([projector_ref[s, g] for g in range(per_slot)], axis=1)
            parts.append(
                lax.dot_general(
                    held[table_ref[0, s]], right, (((0,), (0,)), ((), ())), preferred_element_type=jnp.float32
                )
            )
            places.append([jnp.where(real, table_ref[8 + g, s], patch_tiles) for g in range(per_slot)])
        for part, place in zip(parts, places):
            for g in range(per_slot):
                total[place[g]] += part[:, g * cols : (g + 1) * cols]

    if finish:
        for q in range(patch_tiles):
            out_ref[q] = volume_ref[q].astype(jnp.float32) + (total[q] / column_ref[q]).T


def spread(table, projector, all_cells, lows, chunks, patch_tiles, before, last=()):
    slots, per_slot, rows, cols = projector.shape
    slices = chunks[0].shape[2]
    begin, finish = before is None, bool(last)
    more = ([] if begin else [before]) + list(last) + chunks
    shape = (patch_tiles + 1, slices, cols)
    scratch = [
        pltpu.SMEM(table.shape, jnp.int32),
        pltpu.SemaphoreType.DMA,
        pltpu.SMEM((slots + UNROLL,), jnp.int32),
        pltpu.VMEM((all_cells, rows, slices), jnp.bfloat16),
    ]
    kernel = functools.partial(spread_kernel, lows, begin, finish)
    if not finish:
        inner = kernel
        kernel = lambda *refs: inner(*refs, refs[-5])
    return pl.pallas_call(
        kernel,
        in_specs=[VMEM] * (2 + len(more)),
        out_specs=VMEM,
        out_shape=jax.ShapeDtypeStruct((patch_tiles, cols, slices) if finish else shape, jnp.float32),
        scratch_shapes=scratch + ([pltpu.VMEM(shape, jnp.float32)] if finish else []),
        compiler_params=PARAMS,
        cost_estimate=QUICK,
    )(table, projector, *more)


def gate(value, *after, weight=0):
    return pl.pallas_call(
        lambda *refs: None,
        in_specs=[VMEM] * (1 + len(after)),
        out_specs=VMEM,
        out_shape=jax.ShapeDtypeStruct(value.shape, value.dtype),
        input_output_aliases={0: 0},
        compiler_params=PARAMS,
        cost_estimate=weighs(weight),
    )(value, *after)


def dense_plan(volume, projector, slot_ray, slot_pixel, sinogram, weight_index, weight_table):
    inners = lax.axis_size("inner")
    outers = lax.axis_size("outer")
    tiles = sinogram.shape[0]
    patch_tiles, _, slices = volume.shape
    sizes = (outers, inners, tiles)
    pixel = slot_pixel.T

    turns = sorted(range(inners), key=lambda k: (bin(k).count("1"), k))
    far = [k for k in reversed(turns) if k > 1]
    others = range(1, outers)
    low = lambda j, k: (j * inners + k) * tiles
    arrived = {(j, k): [] for j in range(outers) for k in range(inners)}
    first, *sent = [(j, k) for k in far[:1] for j in others]
    near = [(j, 1) for j in others]
    sent += [(j, k) for k in far[1:] for j in others]
    payload, projector, volume, table = first_send(
        slot_ray, pixel, projector, volume, sizes, low(*first)
    )
    kept = [(0, inners * tiles)] + [(low(j, 0), low(j, 0) + tiles) for j in others]
    sends = {first: payload}
    payloads = further_sums(
        table, projector, volume, tiles, [low(*piece) for piece in near], [], payload
    )
    sends.update(zip(near, payloads))
    kept = [(low(0, 2), low(1, 0)), (0, low(0, 2)), (low(1, 0), low(1, 0) + tiles)]
    *payloads, own = further_sums(
        table, projector, volume, tiles, [low(*piece) for piece in sent], kept[:1], payloads[-1]
    )
    sends.update(zip(sent, payloads))
    for k in far[:1]:
        for j in others:
            arrived[0, k].append(gate(swap(sends[j, k], "outer", j), weight=4))
    for j in others:
        arrived[j, 0].append(swap(sends[j, 1], "inner", 1))
    after = own
    for i, k in enumerate(far):
        bit = k & -k
        after = combine(own, low(0, k) - low(0, 2), tiles, arrived[0, k], after)
        arrived[0, k ^ bit].append(swap(after, "inner", bit) if i == 0 else gate(swap(after, "inner", bit)))
        if i == 0:
            (near_own,) = further_sums(table, projector, volume, tiles, [], kept[1:], after)
            for l in far[1:]:
                for j in others:
                    payload = gate(sends[j, l], after) if LATER else sends[j, l]
                    arrived[0, l].append(swap(payload, "outer", j))
            for j in others:
                after = combine(near_own, 2 * tiles, tiles, arrived[j, 0], after)
                arrived[0, 0].append(swap(after, "outer", j))
    after = combine(near_own, tiles, tiles, [], after)
    arrived[0, 0].append(gate(swap(after, "inner", 1)))
    columns = column_sums(table, projector, patch_tiles, after)
    weights = ray_weights(weight_table, weight_index, slices, columns)
    longest = arrived[0, 0][-2:]
    rest = arrived[0, 0][:-2]
    span = (0, tiles)
    sums = gather(near_own, tiles, [span] * len(longest), longest)
    residual = residual_of(sums, sinogram, weights, tiles, [span] * len(rest), rest)[0]

    chunks = {(0, 0): residual}
    total = None

    def add(pieces, last=()):
        nonlocal total
        total = spread(
            table, projector, outers * inners * tiles, [low(*piece) for piece in pieces],
            [chunks[piece] for piece in pieces], patch_tiles, total, last,
        )

    chunks[0, 2] = swap(residual, "inner", 2)
    chunks[0, 1] = gate(swap(residual, "inner", 1), weight=2)
    chunks[1, 0] = swap(residual, "outer", 1)
    chunks[0, 3] = swap(chunks[0, 2], "inner", 1)
    chunks[1, 2] = swap(chunks[0, 2], "outer", 1)
    done = [(0, 0), (0, 1), (0, 2), (1, 0)]
    add(done)
    chunks[0, 3] = gate(chunks[0, 3], total)
    chunks[1, 3] = swap(chunks[0, 3], "outer", 1)
    chunks[1, 1] = swap(gate(chunks[1, 0], chunks[0, 3]), "inner", 1)
    add([(0, 3), (1, 2)])
    add([(1, 3), (1, 1)], (volume, columns))
    return total


def slot_plan(volume, projector, slot_ray, slot_pixel, sinogram, weight_index, weight_table):
    inners = lax.axis_size("inner")
    outers = lax.axis_size("outer")
    slot_count = projector.shape[0]
    per_slot = projector.shape[1]
    tile_rows = projector.shape[2]
    tile_cols = projector.shape[3]
    patch_tiles = volume.shape[0]
    slice_count = volume.shape[2]
    owned_rows = sinogram.shape[0]
    band_rows = owned_rows * outers
    capacity = 2 * slot_count // inners
    cell_count = inners * capacity
    target = slot_ray // band_rows
    offset = slot_ray % band_rows
    same_target = target[:, None] == target[None, :]
    earlier = jnp.arange(slot_count)[:, None] > jnp.arange(slot_count)[None, :]
    slot_rank = jnp.sum(jnp.logical_and(same_target, earlier), axis=1)
    position = target * capacity + slot_rank
    partial_value = jnp.zeros((slot_count, tile_rows, slice_count), jnp.float32)
    for column in range(per_slot):
        pixels = volume[slot_pixel[:, column]]
        partial_value = partial_value + jnp.einsum(
            "srp,spc->src", projector[:, column], pixels, preferred_element_type=jnp.float32
        )
    outgoing = (
        jnp.zeros((cell_count, tile_rows, slice_count), jnp.float32).at[position].set(partial_value)
    )
    labels = jnp.full((cell_count,), -1.0, jnp.float32).at[position].set(offset.astype(jnp.float32))
    arrived, arrived_rows = (
        lax.all_to_all(
            outgoing.reshape(inners, capacity, tile_rows, slice_count),
            "inner",
            split_axis=0,
            concat_axis=0,
            tiled=True,
        ),
        lax.all_to_all(
            labels.reshape(inners, capacity), "inner", split_axis=0, concat_axis=0, tiled=True
        ),
    )
    selector = (
        jnp.arange(band_rows, dtype=jnp.float32)[:, None] == arrived_rows.reshape(1, cell_count)
    ).astype(jnp.float32)
    block_sums = jnp.dot(
        selector,
        arrived.reshape(cell_count, tile_rows * slice_count),
        precision=lax.Precision.HIGHEST,
    ).reshape(band_rows, tile_rows, slice_count)
    classes = weight_table.shape[0]
    lookup = weight_index[:, :, None] == jnp.arange(classes)[None, None, :]
    weights = jnp.sum(
        jnp.where(lookup, weight_table[None, None, :], jnp.zeros((), weight_table.dtype)), axis=2
    )
    own_sums = lax.psum_scatter(block_sums, "outer", scatter_dimension=0, tiled=True)
    own_residual = (
        weights.astype(jnp.float32)[:, :, None] * (sinogram.astype(jnp.float32) - own_sums)
    ).astype(jnp.bfloat16)
    residual = lax.all_gather(own_residual, "outer", axis=0, tiled=True)
    picked = jnp.dot(
        selector.T.astype(jnp.bfloat16),
        residual.reshape(band_rows, tile_rows * slice_count),
        preferred_element_type=jnp.float32,
    ).astype(jnp.bfloat16)
    returned = lax.all_to_all(
        picked.reshape(inners, capacity, tile_rows, slice_count),
        "inner",
        split_axis=0,
        concat_axis=0,
        tiled=True,
    )
    slot_residual = returned.reshape(cell_count, tile_rows, slice_count)[position]
    owners = jnp.arange(patch_tiles)
    backward_sum = jnp.zeros((patch_tiles, tile_cols, slice_count), jnp.float32)
    column_sum = jnp.zeros((patch_tiles, tile_cols), jnp.float32)
    for column in range(per_slot):
        member = (owners[:, None] == slot_pixel[None, :, column]).astype(jnp.float32)
        spread = jnp.einsum(
            "srp,src->spc", projector[:, column], slot_residual, preferred_element_type=jnp.float32
        )
        backward_sum = backward_sum + jnp.einsum(
            "ts,spc->tpc", member, spread, precision=lax.Precision.HIGHEST
        )
        column_sum = column_sum + jnp.dot(
            member,
            jnp.sum(projector[:, column], axis=1, dtype=jnp.float32),
            precision=lax.Precision.HIGHEST,
        )
    return volume.astype(jnp.float32) + backward_sum / column_sum[:, :, None]


def on_device(volume, projector, slot_ray, slot_pixel, sinogram, weight_index, weight_table):
    inners = lax.axis_size("inner")
    outers = lax.axis_size("outer")
    capacity = 2 * slot_ray.shape[0] // inners
    dense = (inners, outers) == (4, 2) and sinogram.shape[0] * outers <= capacity
    plan = dense_plan if dense else slot_plan
    return plan(volume, projector, slot_ray, slot_pixel, sinogram, weight_index, weight_table)


def solution(mesh):
    in_specs = (
        P(("group", "inner", "outer"), None, "cuts"),
        P(("inner", "outer"), None, None, None),
        P(("inner", "outer")),
        P(("inner", "outer"), None),
        P(("group", "inner", "outer"), None, "cuts"),
        P(("group", "inner", "outer"), None),
        P(),
    )
    out_specs = P(("group", "inner", "outer"), None, "cuts")
    return jax.shard_map(
        on_device, mesh=mesh, in_specs=in_specs, out_specs=out_specs, check_vma=False
    )
```

```python
import functools
import math

import jax
import jax.numpy as jnp
from jax import lax
from jax.experimental import pallas as pl
from jax.experimental.pallas import tpu as pltpu
from jax.sharding import PartitionSpec as P

FULL = 32700.0
UNROLL = 4
LATER = True
VMEM = pl.BlockSpec(memory_space=pltpu.VMEM)
SMEM = pl.BlockSpec(memory_space=pltpu.SMEM)
HBM = pl.BlockSpec(memory_space=pltpu.HBM)
ANY = pl.BlockSpec(memory_space=pl.ANY)


def weighs(weight):
    return pl.CostEstimate(flops=max(int(weight * 1e9), 1), bytes_accessed=1, transcendentals=0)


QUICK = weighs(0)
PARAMS = pltpu.CompilerParams(vmem_limit_bytes=24 * 2**20)


def round_up(value, step):
    return -(-value // step) * step


def swap(value, axis, bits):
    size = lax.axis_size(axis)
    return lax.ppermute(value, axis, [(i, i ^ bits) for i in range(size)])


def pack(tile, out_ref, levels_ref, t):
    rows = tile.shape[0]
    top = jnp.maximum(jnp.max(jnp.abs(tile), axis=0, keepdims=True), 1e-30)
    level = jnp.ceil(jnp.log2(top))
    out_ref[t * rows : (t + 1) * rows, :] = (
        jnp.round(tile * (FULL * jnp.exp2(-level))).astype(jnp.int32).astype(jnp.int16)
    )
    levels_ref[t : t + 1, :] = level


def unpack(ref, scale, t, rows):
    block = ref[t * rows : (t + 1) * rows, :]
    return block.astype(jnp.int32).astype(jnp.float32) * scale[t : t + 1, :]


def scales(ref, tiles, rows):
    raw = ref[tiles * rows :, :].astype(jnp.int32).astype(jnp.float32)
    return jnp.exp2(raw) * (1.0 / FULL)


def payload_of(tiles, rows, slices):
    return jax.ShapeDtypeStruct((tiles * rows + round_up(tiles, 16), slices), jnp.int16)


def split(value, size):
    if size & (size - 1) == 0:
        return lax.shift_right_logical(value, size.bit_length() - 1), value & (size - 1)
    return lax.div(value, size), lax.rem(value, size)


def cell_of(ray, zi, xi, tiles, outers, inners):
    owner, tile = split(ray, tiles)
    inner, outer = split(owner, outers)
    return ((outer ^ xi) * inners + (inner ^ zi)) * tiles + tile


def place_slots(pos, ray_ref, cell_ref, sizes):
    outers, inners, tiles = sizes

    @pl.loop(0, ray_ref.shape[0], unroll=4)
    def _(s):
        cell_ref[s] = cell_of(ray_ref[s], pos[0], pos[1], tiles, outers, inners)


def list_slots(cell_ref, slots, ranges, slot_list):
    def look(s, count):
        slot_list[count] = s
        cell = cell_ref[s]
        hit = jnp.bool_(False)
        for low, high in ranges:
            hit = hit | ((cell >= low) & (cell < high))
        return count + hit.astype(jnp.int32)

    return lax.fori_loop(slots[0], slots[1], look, jnp.int32(0), unroll=4)


def project(count, together, low, spare, slot_list, cell_ref, pixel_ref, projector_ref, volume_ref, total):
    per_slot = projector_ref.shape[1]

    @pl.loop(0, (count + together - 1) // together)
    def _(i):
        parts, places = [], []
        for u in range(together):
            at = i * together + u
            real = at < count
            s = jnp.where(real, slot_list[at], 0)
            left = jnp.concatenate([projector_ref[s, g] for g in range(per_slot)], axis=1)
            right = jnp.concatenate([volume_ref[pixel_ref[g, s]] for g in range(per_slot)], axis=0)
            parts.append(jnp.dot(left, right, preferred_element_type=jnp.float32))
            places.append(jnp.where(real, cell_ref[s] - low, spare))
        for place, part in zip(places, parts):
            total[place] += part


def joined(tile, t, arrived):
    rows = tile.shape[0]
    for ref, first, count, factor in arrived:
        if first <= t < first + count:
            tile = tile + unpack(ref, factor, t - first, rows)
    return tile


def with_scales(refs, spans, rows):
    return [(ref, first, count, scales(ref, count, rows)) for ref, (first, count) in zip(refs, spans)]


def send_out(total, base, tiles, arrived, send, levels):
    rows = total.shape[1]
    levels[...] = jnp.zeros_like(levels)
    for t in range(tiles):
        pack(joined(total[base + t], t, arrived), send, levels, t)
    send[tiles * rows :, :] = levels[...].astype(jnp.int32).astype(jnp.int16)


def first_kernel(
    sizes, low, ray_hbm, pixel_hbm, projector_hbm, volume_hbm,
    send, projector_ref, volume_ref, out_ref, ray_ref, table_ref, slot_list, total, levels, sems,
):
    slots = ray_ref.shape[0]
    tiles = sizes[2]
    blocks = sems.shape[0] - 4
    cell_ref, pixel_ref = table_ref.at[0], table_ref.at[pl.ds(8, pixel_hbm.shape[0])]
    block = slots // blocks
    pairs = [(ray_hbm, ray_ref), (pixel_hbm, pixel_ref), (volume_hbm, volume_ref)]
    for b in range(blocks):
        span = pl.ds(b * block, block)
        pairs.append((projector_hbm.at[span], projector_ref.at[span]))
    copies = [
        pltpu.make_async_copy(source, target, sems.at[i]) for i, (source, target) in enumerate(pairs)
    ]
    for copy in copies:
        copy.start()
    total[...] = jnp.zeros_like(total)
    copies[0].wait()
    place_slots((lax.axis_index("inner"), lax.axis_index("outer")), ray_ref, cell_ref, sizes)
    copies[1].wait()
    table_copy = pltpu.make_async_copy(table_ref, out_ref, sems.at[3 + blocks])
    table_copy.start()
    copies[2].wait()
    for b in range(blocks):
        count = list_slots(cell_ref, (b * block, b * block + block), [(low, low + tiles)], slot_list)
        copies[3 + b].wait()
        project(
            count, 4, low, tiles, slot_list, cell_ref, pixel_ref, projector_ref, volume_ref, total
        )
    send_out(total, 0, tiles, [], send, levels)
    table_copy.wait()


def hold(value):
    return pltpu.with_memory_space_constraint(value, pltpu.HBM)


def first_send(slot_ray, pixel, projector, volume, sizes, low):
    slots, per_slot, rows, cols = projector.shape
    tiles = sizes[2]
    table = (8 + per_slot, slots)
    slices = volume.shape[2]
    return pl.pallas_call(
        functools.partial(first_kernel, sizes, low),
        in_specs=[HBM, HBM, HBM, HBM],
        out_specs=[VMEM, VMEM, VMEM, VMEM],
        out_shape=[
            payload_of(tiles, rows, slices),
            jax.ShapeDtypeStruct(projector.shape, projector.dtype),
            jax.ShapeDtypeStruct(volume.shape, volume.dtype),
            jax.ShapeDtypeStruct(table, jnp.int32),
        ],
        scratch_shapes=[
            pltpu.SMEM(slot_ray.shape, jnp.int32),
            pltpu.SMEM(table, jnp.int32),
            pltpu.SMEM((slots + UNROLL,), jnp.int32),
            pltpu.VMEM((tiles + 1, rows, slices), jnp.float32),
            pltpu.VMEM((round_up(tiles, 16), slices), jnp.float32),
            pltpu.SemaphoreType.DMA((4 + math.gcd(slots, 4),)),
        ],
        compiler_params=pltpu.CompilerParams(vmem_limit_bytes=48 * 2**20),
        cost_estimate=QUICK,
    )(hold(slot_ray), hold(pixel), hold(projector), hold(volume))


def further_kernel(tiles, sent, ranges, table_from, projector_ref, volume_ref, after, *rest):
    sends = rest[: len(sent)]
    *own_ref, table_ref, sem, slot_list, total, levels = rest[len(sent) :]
    copy = pltpu.make_async_copy(table_from, table_ref, sem)
    copy.start()
    for ref in own_ref:
        ref[...] = jnp.zeros_like(ref)
    copy.wait()
    slots, per_slot = projector_ref.shape[:2]
    cell_ref, pixel_ref = table_ref.at[0], table_ref.at[pl.ds(8, per_slot)]
    for send, low in zip(sends, sent):
        total[...] = jnp.zeros_like(total)
        count = list_slots(cell_ref, (0, slots), [(low, low + tiles)], slot_list)
        project(
            count, 2, low, tiles, slot_list, cell_ref, pixel_ref, projector_ref, volume_ref, total
        )
        send_out(total, 0, tiles, [], send, levels)
    base = 0
    for ref in own_ref:
        for low, high in ranges:
            count = list_slots(cell_ref, (0, slots), [(low, high)], slot_list)
            project(
                count, UNROLL, low - base, ref.shape[0] - 1, slot_list, cell_ref, pixel_ref,
                projector_ref, volume_ref, ref,
            )
            base += high - low


def further_sums(table, projector, volume, tiles, sent, ranges, after):
    slots, per_slot, rows, cols = projector.shape
    slices = volume.shape[2]
    kept = sum(high - low for low, high in ranges)
    out_shape = [payload_of(tiles, rows, slices)] * len(sent)
    if kept:
        out_shape.append(jax.ShapeDtypeStruct((kept + 1, rows, slices), jnp.float32))
    return pl.pallas_call(
        functools.partial(further_kernel, tiles, sent, ranges),
        in_specs=[VMEM, VMEM, VMEM, ANY],
        out_specs=[VMEM] * len(out_shape),
        out_shape=out_shape,
        scratch_shapes=[
            pltpu.SMEM(table.shape, jnp.int32),
            pltpu.SemaphoreType.DMA,
            pltpu.SMEM((slots + UNROLL,), jnp.int32),
            pltpu.VMEM((tiles + 1, rows, slices), jnp.float32),
            pltpu.VMEM((round_up(tiles, 16), slices), jnp.float32),
        ],
        compiler_params=PARAMS,
        cost_estimate=QUICK,
    )(table, projector, volume, after)


def combine_kernel(low, part, spans, own_ref, after, *rest):
    refs, (out_ref, levels) = rest[: len(spans)], rest[len(spans) :]
    send_out(own_ref, low, part, with_scales(refs, spans, own_ref.shape[1]), out_ref, levels)


def combine(own, low, part, arrived, after):
    _, rows, slices = own.shape
    return pl.pallas_call(
        functools.partial(combine_kernel, low, part, [(0, part)] * len(arrived)),
        in_specs=[VMEM, ANY] + [VMEM] * len(arrived),
        out_specs=VMEM,
        out_shape=payload_of(part, rows, slices),
        scratch_shapes=[pltpu.VMEM((round_up(part, 16), slices), jnp.float32)],
        compiler_params=PARAMS,
        cost_estimate=QUICK,
    )(own, after, *arrived)


def gather_kernel(spans, own_ref, *rest):
    refs, out_ref = rest[: len(spans)], rest[len(spans)]
    arrived = with_scales(refs, spans, own_ref.shape[1])
    for t in range(out_ref.shape[0]):
        out_ref[t] = joined(own_ref[t], t, arrived)


def gather(own, tiles, spans, arrived):
    return pl.pallas_call(
        functools.partial(gather_kernel, spans),
        in_specs=[VMEM] * (1 + len(arrived)),
        out_specs=VMEM,
        out_shape=jax.ShapeDtypeStruct((tiles,) + own.shape[1:], jnp.float32),
        compiler_params=PARAMS,
        cost_estimate=QUICK,
    )(own, *arrived)


def weight_kernel(table_ref, index_ref, after, out_ref):
    looked = jnp.zeros(index_ref.shape, jnp.float32)
    for c in range(table_ref.shape[0]):
        looked = jnp.where(index_ref[...] == c, table_ref[c], looked)
    for t in range(index_ref.shape[0]):
        wide = jnp.broadcast_to(looked[t : t + 1, :], (out_ref.shape[2], out_ref.shape[1]))
        out_ref[t] = wide.T.astype(jnp.bfloat16)


def ray_weights(table, index, slices, after):
    tiles, rows = index.shape
    return pl.pallas_call(
        weight_kernel,
        in_specs=[SMEM, VMEM, ANY],
        out_specs=VMEM,
        out_shape=jax.ShapeDtypeStruct((tiles, rows, slices), jnp.bfloat16),
        compiler_params=PARAMS,
        cost_estimate=QUICK,
    )(table.astype(jnp.float32), index, after)


def residual_kernel(spans, sum_ref, sinogram_ref, weight_ref, *rest):
    refs, out_refs = rest[: len(spans)], rest[len(spans) :]
    arrived = with_scales(refs, spans, sum_ref.shape[1])
    part = out_refs[0].shape[0]
    for t in range(sum_ref.shape[0]):
        gap = sinogram_ref[t].astype(jnp.float32) - joined(sum_ref[t], t, arrived)
        out_refs[t // part][t % part] = (weight_ref[t].astype(jnp.float32) * gap).astype(
            jnp.bfloat16
        )


def residual_of(sums, sinogram, weights, part, spans, arrived):
    tiles, rows, slices = sinogram.shape
    return pl.pallas_call(
        functools.partial(residual_kernel, spans),
        in_specs=[VMEM] * (3 + len(arrived)),
        out_specs=[VMEM] * (tiles // part),
        out_shape=[jax.ShapeDtypeStruct((part, rows, slices), jnp.bfloat16)] * (tiles // part),
        compiler_params=PARAMS,
        cost_estimate=QUICK,
    )(sums, sinogram, weights, *arrived)


def column_kernel(table_ref, projector_ref, after, out_ref):
    slots, per_slot, rows, cols = projector_ref.shape
    out_ref[...] = jnp.zeros_like(out_ref)

    @pl.loop(0, slots)
    def _(s):
        for g in range(per_slot):
            column = jnp.sum(projector_ref[s, g].astype(jnp.float32), axis=0, keepdims=True)
            out_ref[table_ref[8 + g, s]] += column

    out_ref[...] = 1.0 / out_ref[...]


def column_sums(table, projector, patch_tiles, after):
    slots, per_slot, rows, cols = projector.shape
    return pl.pallas_call(
        column_kernel,
        in_specs=[SMEM, VMEM, ANY],
        out_specs=VMEM,
        out_shape=jax.ShapeDtypeStruct((patch_tiles, 1, cols), jnp.float32),
        compiler_params=PARAMS,
        cost_estimate=QUICK,
    )(table, projector, after)


def spread_kernel(lows, begin, finish, table_from, projector_ref, *rest):
    rest = list(rest)
    before = None if begin else rest.pop(0)
    volume_ref, column_ref = (rest.pop(0), rest.pop(0)) if finish else (None, None)
    chunks, (out_ref, table_ref, sem, slot_list, held) = rest[: len(lows)], rest[len(lows) : len(lows) + 5]
    total = rest[-1]
    copy = pltpu.make_async_copy(table_from, table_ref, sem)
    copy.start()
    slots, per_slot, rows, cols = projector_ref.shape
    part = chunks[0].shape[0]
    patch_tiles = total.shape[0] - 1
    for low, chunk in zip(lows, chunks):
        held[low : low + part] = chunk[...]
    if begin:
        total[...] = jnp.zeros_like(total)
    else:
        total[...] = before[...]
    copy.wait()
    count = list_slots(table_ref.at[0], (0, slots), [(low, low + part) for low in lows], slot_list)

    @pl.loop(0, (count + UNROLL - 1) // UNROLL)
    def _(i):
        parts, places = [], []
        for u in range(UNROLL):
            real = i * UNROLL + u < count
            s = jnp.where(real, slot_list[i * UNROLL + u], slot_list[0])
            right = jnp.concatenate([projector_ref[s, g] for g in range(per_slot)], axis=1)
            parts.append(
                lax.dot_general(
                    held[table_ref[0, s]], right, (((0,), (0,)), ((), ())), preferred_element_type=jnp.float32
                )
            )
            places.append([jnp.where(real, table_ref[8 + g, s], patch_tiles) for g in range(per_slot)])
        for part, place in zip(parts, places):
            for g in range(per_slot):
                total[place[g]] += part[:, g * cols : (g + 1) * cols]

    if finish:
        for q in range(patch_tiles):
            out_ref[q] = volume_ref[q].astype(jnp.float32) + (total[q] * column_ref[q]).T


def spread(table, projector, all_cells, lows, chunks, patch_tiles, before, last=()):
    slots, per_slot, rows, cols = projector.shape
    slices = chunks[0].shape[2]
    begin, finish = before is None, bool(last)
    more = ([] if begin else [before]) + list(last) + chunks
    shape = (patch_tiles + 1, slices, cols)
    scratch = [
        pltpu.SMEM(table.shape, jnp.int32),
        pltpu.SemaphoreType.DMA,
        pltpu.SMEM((slots + UNROLL,), jnp.int32),
        pltpu.VMEM((all_cells, rows, slices), jnp.bfloat16),
    ]
    kernel = functools.partial(spread_kernel, lows, begin, finish)
    if not finish:
        inner = kernel
        kernel = lambda *refs: inner(*refs, refs[-5])
    return pl.pallas_call(
        kernel,
        in_specs=[VMEM] * (2 + len(more)),
        out_specs=VMEM,
        out_shape=jax.ShapeDtypeStruct((patch_tiles, cols, slices) if finish else shape, jnp.float32),
        scratch_shapes=scratch + ([pltpu.VMEM(shape, jnp.float32)] if finish else []),
        compiler_params=PARAMS,
        cost_estimate=QUICK,
    )(table, projector, *more)


def gate(value, *after, weight=0):
    return pl.pallas_call(
        lambda *refs: None,
        in_specs=[VMEM] * (1 + len(after)),
        out_specs=VMEM,
        out_shape=jax.ShapeDtypeStruct(value.shape, value.dtype),
        input_output_aliases={0: 0},
        compiler_params=PARAMS,
        cost_estimate=weighs(weight),
    )(value, *after)


def dense_plan(volume, projector, slot_ray, slot_pixel, sinogram, weight_index, weight_table):
    inners = lax.axis_size("inner")
    outers = lax.axis_size("outer")
    tiles = sinogram.shape[0]
    patch_tiles, _, slices = volume.shape
    sizes = (outers, inners, tiles)
    pixel = slot_pixel.T

    turns = sorted(range(inners), key=lambda k: (bin(k).count("1"), k))
    far = [k for k in reversed(turns) if k > 1]
    others = range(1, outers)
    low = lambda j, k: (j * inners + k) * tiles
    arrived = {(j, k): [] for j in range(outers) for k in range(inners)}
    first, *sent = [(j, k) for k in far[:1] for j in others]
    near = [(j, 1) for j in others]
    sent += [(j, k) for k in far[1:] for j in others]
    payload, projector, volume, table = first_send(
        slot_ray, pixel, projector, volume, sizes, low(*first)
    )
    kept = [(0, inners * tiles)] + [(low(j, 0), low(j, 0) + tiles) for j in others]
    sends = {first: payload}
    payloads = further_sums(
        table, projector, volume, tiles, [low(*piece) for piece in near], [], payload
    )
    sends.update(zip(near, payloads))
    kept = [(low(0, 2), low(1, 0)), (0, low(0, 2)), (low(1, 0), low(1, 0) + tiles)]
    *payloads, own = further_sums(
        table, projector, volume, tiles, [low(*piece) for piece in sent], kept[:1], payloads[-1]
    )
    sends.update(zip(sent, payloads))
    for k in far[:1]:
        for j in others:
            arrived[0, k].append(gate(swap(sends[j, k], "outer", j), weight=4))
    for j in others:
        arrived[j, 0].append(swap(sends[j, 1], "inner", 1))
    after = own
    for i, k in enumerate(far):
        bit = k & -k
        after = combine(own, low(0, k) - low(0, 2), tiles, arrived[0, k], after)
        arrived[0, k ^ bit].append(swap(after, "inner", bit) if i == 0 else gate(swap(after, "inner", bit)))
        if i == 0:
            (near_own,) = further_sums(table, projector, volume, tiles, [], kept[1:], after)
            for l in far[1:]:
                for j in others:
                    payload = gate(sends[j, l], after) if LATER else sends[j, l]
                    arrived[0, l].append(swap(payload, "outer", j))
            for j in others:
                after = combine(near_own, 2 * tiles, tiles, arrived[j, 0], after)
                arrived[0, 0].append(swap(after, "outer", j))
    after = combine(near_own, tiles, tiles, [], after)
    arrived[0, 0].append(gate(swap(after, "inner", 1)))
    columns = column_sums(table, projector, patch_tiles, after)
    weights = ray_weights(weight_table, weight_index, slices, columns)
    longest = arrived[0, 0][-2:]
    rest = arrived[0, 0][:-2]
    span = (0, tiles)
    sums = gather(near_own, tiles, [span] * len(longest), longest)
    residual = residual_of(sums, sinogram, weights, tiles, [span] * len(rest), rest)[0]

    chunks = {(0, 0): residual}
    total = None

    def add(pieces, last=()):
        nonlocal total
        total = spread(
            table, projector, outers * inners * tiles, [low(*piece) for piece in pieces],
            [chunks[piece] for piece in pieces], patch_tiles, total, last,
        )

    chunks[0, 2] = swap(residual, "inner", 2)
    chunks[0, 1] = gate(swap(residual, "inner", 1), weight=2)
    chunks[1, 0] = swap(residual, "outer", 1)
    chunks[0, 3] = swap(chunks[0, 2], "inner", 1)
    chunks[1, 2] = swap(chunks[0, 2], "outer", 1)
    done = [(0, 0), (0, 1), (0, 2), (1, 0)]
    add(done)
    chunks[0, 3] = gate(chunks[0, 3], total)
    chunks[1, 3] = swap(chunks[0, 3], "outer", 1)
    chunks[1, 1] = swap(gate(chunks[1, 0], chunks[0, 3]), "inner", 1)
    add([(0, 3), (1, 2)])
    add([(1, 3), (1, 1)], (volume, columns))
    return total


def slot_plan(volume, projector, slot_ray, slot_pixel, sinogram, weight_index, weight_table):
    inners = lax.axis_size("inner")
    outers = lax.axis_size("outer")
    slot_count = projector.shape[0]
    per_slot = projector.shape[1]
    tile_rows = projector.shape[2]
    tile_cols = projector.shape[3]
    patch_tiles = volume.shape[0]
    slice_count = volume.shape[2]
    owned_rows = sinogram.shape[0]
    band_rows = owned_rows * outers
    capacity = 2 * slot_count // inners
    cell_count = inners * capacity
    target = slot_ray // band_rows
    offset = slot_ray % band_rows
    same_target = target[:, None] == target[None, :]
    earlier = jnp.arange(slot_count)[:, None] > jnp.arange(slot_count)[None, :]
    slot_rank = jnp.sum(jnp.logical_and(same_target, earlier), axis=1)
    position = target * capacity + slot_rank
    partial_value = jnp.zeros((slot_count, tile_rows, slice_count), jnp.float32)
    for column in range(per_slot):
        pixels = volume[slot_pixel[:, column]]
        partial_value = partial_value + jnp.einsum(
            "srp,spc->src", projector[:, column], pixels, preferred_element_type=jnp.float32
        )
    outgoing = (
        jnp.zeros((cell_count, tile_rows, slice_count), jnp.float32).at[position].set(partial_value)
    )
    labels = jnp.full((cell_count,), -1.0, jnp.float32).at[position].set(offset.astype(jnp.float32))
    arrived, arrived_rows = (
        lax.all_to_all(
            outgoing.reshape(inners, capacity, tile_rows, slice_count),
            "inner",
            split_axis=0,
            concat_axis=0,
            tiled=True,
        ),
        lax.all_to_all(
            labels.reshape(inners, capacity), "inner", split_axis=0, concat_axis=0, tiled=True
        ),
    )
    selector = (
        jnp.arange(band_rows, dtype=jnp.float32)[:, None] == arrived_rows.reshape(1, cell_count)
    ).astype(jnp.float32)
    block_sums = jnp.dot(
        selector,
        arrived.reshape(cell_count, tile_rows * slice_count),
        precision=lax.Precision.HIGHEST,
    ).reshape(band_rows, tile_rows, slice_count)
    classes = weight_table.shape[0]
    lookup = weight_index[:, :, None] == jnp.arange(classes)[None, None, :]
    weights = jnp.sum(
        jnp.where(lookup, weight_table[None, None, :], jnp.zeros((), weight_table.dtype)), axis=2
    )
    own_sums = lax.psum_scatter(block_sums, "outer", scatter_dimension=0, tiled=True)
    own_residual = (
        weights.astype(jnp.float32)[:, :, None] * (sinogram.astype(jnp.float32) - own_sums)
    ).astype(jnp.bfloat16)
    residual = lax.all_gather(own_residual, "outer", axis=0, tiled=True)
    picked = jnp.dot(
        selector.T.astype(jnp.bfloat16),
        residual.reshape(band_rows, tile_rows * slice_count),
        preferred_element_type=jnp.float32,
    ).astype(jnp.bfloat16)
    returned = lax.all_to_all(
        picked.reshape(inners, capacity, tile_rows, slice_count),
        "inner",
        split_axis=0,
        concat_axis=0,
        tiled=True,
    )
    slot_residual = returned.reshape(cell_count, tile_rows, slice_count)[position]
    owners = jnp.arange(patch_tiles)
    backward_sum = jnp.zeros((patch_tiles, tile_cols, slice_count), jnp.float32)
    column_sum = jnp.zeros((patch_tiles, tile_cols), jnp.float32)
    for column in range(per_slot):
        member = (owners[:, None] == slot_pixel[None, :, column]).astype(jnp.float32)
        spread = jnp.einsum(
            "srp,src->spc", projector[:, column], slot_residual, preferred_element_type=jnp.float32
        )
        backward_sum = backward_sum + jnp.einsum(
            "ts,spc->tpc", member, spread, precision=lax.Precision.HIGHEST
        )
        column_sum = column_sum + jnp.dot(
            member,
            jnp.sum(projector[:, column], axis=1, dtype=jnp.float32),
            precision=lax.Precision.HIGHEST,
        )
    return volume.astype(jnp.float32) + backward_sum / column_sum[:, :, None]


def on_device(volume, projector, slot_ray, slot_pixel, sinogram, weight_index, weight_table):
    inners = lax.axis_size("inner")
    outers = lax.axis_size("outer")
    capacity = 2 * slot_ray.shape[0] // inners
    dense = (inners, outers) == (4, 2) and sinogram.shape[0] * outers <= capacity
    plan = dense_plan if dense else slot_plan
    return plan(volume, projector, slot_ray, slot_pixel, sinogram, weight_index, weight_table)


def solution(mesh):
    in_specs = (
        P(("group", "inner", "outer"), None, "cuts"),
        P(("inner", "outer"), None, None, None),
        P(("inner", "outer")),
        P(("inner", "outer"), None),
        P(("group", "inner", "outer"), None, "cuts"),
        P(("group", "inner", "outer"), None),
        P(),
    )
    out_specs = P(("group", "inner", "outer"), None, "cuts")
    return jax.shard_map(
        on_device, mesh=mesh, in_specs=in_specs, out_specs=out_specs, check_vma=False
    )
```

```python
import functools
import math

import jax
import jax.numpy as jnp
from jax import lax
from jax.experimental import pallas as pl
from jax.experimental.pallas import tpu as pltpu
from jax.sharding import PartitionSpec as P

FULL = 32700.0
UNROLL = 4
LATER = True
VMEM = pl.BlockSpec(memory_space=pltpu.VMEM)
SMEM = pl.BlockSpec(memory_space=pltpu.SMEM)
HBM = pl.BlockSpec(memory_space=pltpu.HBM)
ANY = pl.BlockSpec(memory_space=pl.ANY)


def weighs(weight):
    return pl.CostEstimate(flops=max(int(weight * 1e9), 1), bytes_accessed=1, transcendentals=0)


QUICK = weighs(0)
PARAMS = pltpu.CompilerParams(vmem_limit_bytes=24 * 2**20)


def round_up(value, step):
    return -(-value // step) * step


def swap(value, axis, bits):
    size = lax.axis_size(axis)
    return lax.ppermute(value, axis, [(i, i ^ bits) for i in range(size)])


def pack(tile, out_ref, levels_ref, t):
    rows = tile.shape[0]
    top = jnp.maximum(jnp.max(jnp.abs(tile), axis=0, keepdims=True), 1e-30)
    level = jnp.ceil(jnp.log2(top))
    out_ref[t * rows : (t + 1) * rows, :] = (
        jnp.round(tile * (FULL * jnp.exp2(-level))).astype(jnp.int32).astype(jnp.int16)
    )
    levels_ref[t : t + 1, :] = level


def unpack(ref, scale, t, rows):
    block = ref[t * rows : (t + 1) * rows, :]
    return block.astype(jnp.int32).astype(jnp.float32) * scale[t : t + 1, :]


def scales(ref, tiles, rows):
    raw = ref[tiles * rows :, :].astype(jnp.int32).astype(jnp.float32)
    return jnp.exp2(raw) * (1.0 / FULL)


def payload_of(tiles, rows, slices):
    return jax.ShapeDtypeStruct((tiles * rows + round_up(tiles, 16), slices), jnp.int16)


def split(value, size):
    if size & (size - 1) == 0:
        return lax.shift_right_logical(value, size.bit_length() - 1), value & (size - 1)
    return lax.div(value, size), lax.rem(value, size)


def cell_of(ray, zi, xi, tiles, outers, inners):
    owner, tile = split(ray, tiles)
    inner, outer = split(owner, outers)
    return ((outer ^ xi) * inners + (inner ^ zi)) * tiles + tile


def place_slots(pos, ray_ref, cell_ref, sizes):
    outers, inners, tiles = sizes

    @pl.loop(0, ray_ref.shape[0], unroll=4)
    def _(s):
        cell_ref[s] = cell_of(ray_ref[s], pos[0], pos[1], tiles, outers, inners)


def list_slots(cell_ref, slots, ranges, slot_list):
    def look(s, count):
        slot_list[count] = s
        cell = cell_ref[s]
        hit = jnp.bool_(False)
        for low, high in ranges:
            hit = hit | ((cell >= low) & (cell < high))
        return count + hit.astype(jnp.int32)

    return lax.fori_loop(slots[0], slots[1], look, jnp.int32(0), unroll=4)


def project(count, together, low, spare, slot_list, cell_ref, pixel_ref, projector_ref, volume_ref, total):
    per_slot = projector_ref.shape[1]

    @pl.loop(0, (count + together - 1) // together)
    def _(i):
        parts, places = [], []
        for u in range(together):
            at = i * together + u
            real = at < count
            s = jnp.where(real, slot_list[at], 0)
            left = jnp.concatenate([projector_ref[s, g] for g in range(per_slot)], axis=1)
            right = jnp.concatenate([volume_ref[pixel_ref[g, s]] for g in range(per_slot)], axis=0)
            parts.append(jnp.dot(left, right, preferred_element_type=jnp.float32))
            places.append(jnp.where(real, cell_ref[s] - low, spare))
        for place, part in zip(places, parts):
            total[place] += part


def joined(tile, t, arrived):
    rows = tile.shape[0]
    for ref, first, count, factor in arrived:
        if first <= t < first + count:
            tile = tile + unpack(ref, factor, t - first, rows)
    return tile


def with_scales(refs, spans, rows):
    return [(ref, first, count, scales(ref, count, rows)) for ref, (first, count) in zip(refs, spans)]


def send_out(total, base, tiles, arrived, send, levels):
    rows = total.shape[1]
    levels[...] = jnp.zeros_like(levels)
    for t in range(tiles):
        pack(joined(total[base + t], t, arrived), send, levels, t)
    send[tiles * rows :, :] = levels[...].astype(jnp.int32).astype(jnp.int16)


def first_kernel(
    sizes, low, ray_hbm, pixel_hbm, projector_hbm, volume_hbm,
    send, projector_ref, volume_ref, out_ref, ray_ref, table_ref, slot_list, total, levels, sems,
):
    slots = ray_ref.shape[0]
    tiles = sizes[2]
    blocks = sems.shape[0] - 4
    cell_ref, pixel_ref = table_ref.at[0], table_ref.at[pl.ds(8, pixel_hbm.shape[0])]
    block = slots // blocks
    pairs = [(ray_hbm, ray_ref), (pixel_hbm, pixel_ref), (volume_hbm, volume_ref)]
    for b in range(blocks):
        span = pl.ds(b * block, block)
        pairs.append((projector_hbm.at[span], projector_ref.at[span]))
    copies = [
        pltpu.make_async_copy(source, target, sems.at[i]) for i, (source, target) in enumerate(pairs)
    ]
    for copy in copies:
        copy.start()
    total[...] = jnp.zeros_like(total)
    copies[0].wait()
    place_slots((lax.axis_index("inner"), lax.axis_index("outer")), ray_ref, cell_ref, sizes)
    copies[1].wait()
    table_copy = pltpu.make_async_copy(table_ref, out_ref, sems.at[3 + blocks])
    table_copy.start()
    copies[2].wait()
    for b in range(blocks):
        count = list_slots(cell_ref, (b * block, b * block + block), [(low, low + tiles)], slot_list)
        copies[3 + b].wait()
        project(
            count, 2, low, tiles, slot_list, cell_ref, pixel_ref, projector_ref, volume_ref, total
        )
    send_out(total, 0, tiles, [], send, levels)
    table_copy.wait()


def hold(value):
    return pltpu.with_memory_space_constraint(value, pltpu.HBM)


def first_send(slot_ray, pixel, projector, volume, sizes, low):
    slots, per_slot, rows, cols = projector.shape
    tiles = sizes[2]
    table = (8 + per_slot, slots)
    slices = volume.shape[2]
    return pl.pallas_call(
        functools.partial(first_kernel, sizes, low),
        in_specs=[HBM, HBM, HBM, HBM],
        out_specs=[VMEM, VMEM, VMEM, VMEM],
        out_shape=[
            payload_of(tiles, rows, slices),
            jax.ShapeDtypeStruct(projector.shape, projector.dtype),
            jax.ShapeDtypeStruct(volume.shape, volume.dtype),
            jax.ShapeDtypeStruct(table, jnp.int32),
        ],
        scratch_shapes=[
            pltpu.SMEM(slot_ray.shape, jnp.int32),
            pltpu.SMEM(table, jnp.int32),
            pltpu.SMEM((slots + UNROLL,), jnp.int32),
            pltpu.VMEM((tiles + 1, rows, slices), jnp.float32),
            pltpu.VMEM((round_up(tiles, 16), slices), jnp.float32),
            pltpu.SemaphoreType.DMA((4 + math.gcd(slots, 4),)),
        ],
        compiler_params=pltpu.CompilerParams(vmem_limit_bytes=48 * 2**20),
        cost_estimate=QUICK,
    )(hold(slot_ray), hold(pixel), hold(projector), hold(volume))


def further_kernel(tiles, sent, ranges, table_from, projector_ref, volume_ref, after, *rest):
    sends = rest[: len(sent)]
    *own_ref, table_ref, sem, slot_list, total, levels = rest[len(sent) :]
    copy = pltpu.make_async_copy(table_from, table_ref, sem)
    copy.start()
    for ref in own_ref:
        ref[...] = jnp.zeros_like(ref)
    copy.wait()
    slots, per_slot = projector_ref.shape[:2]
    cell_ref, pixel_ref = table_ref.at[0], table_ref.at[pl.ds(8, per_slot)]
    for send, low in zip(sends, sent):
        total[...] = jnp.zeros_like(total)
        count = list_slots(cell_ref, (0, slots), [(low, low + tiles)], slot_list)
        project(
            count, 2, low, tiles, slot_list, cell_ref, pixel_ref, projector_ref, volume_ref, total
        )
        send_out(total, 0, tiles, [], send, levels)
    base = 0
    for ref in own_ref:
        for low, high in ranges:
            count = list_slots(cell_ref, (0, slots), [(low, high)], slot_list)
            project(
                count, UNROLL, low - base, ref.shape[0] - 1, slot_list, cell_ref, pixel_ref,
                projector_ref, volume_ref, ref,
            )
            base += high - low


def further_sums(table, projector, volume, tiles, sent, ranges, after):
    slots, per_slot, rows, cols = projector.shape
    slices = volume.shape[2]
    kept = sum(high - low for low, high in ranges)
    out_shape = [payload_of(tiles, rows, slices)] * len(sent)
    if kept:
        out_shape.append(jax.ShapeDtypeStruct((kept + 1, rows, slices), jnp.float32))
    return pl.pallas_call(
        functools.partial(further_kernel, tiles, sent, ranges),
        in_specs=[VMEM, VMEM, VMEM, ANY],
        out_specs=[VMEM] * len(out_shape),
        out_shape=out_shape,
        scratch_shapes=[
            pltpu.SMEM(table.shape, jnp.int32),
            pltpu.SemaphoreType.DMA,
            pltpu.SMEM((slots + UNROLL,), jnp.int32),
            pltpu.VMEM((tiles + 1, rows, slices), jnp.float32),
            pltpu.VMEM((round_up(tiles, 16), slices), jnp.float32),
        ],
        compiler_params=PARAMS,
        cost_estimate=QUICK,
    )(table, projector, volume, after)


def combine_kernel(low, part, spans, own_ref, after, *rest):
    refs, (out_ref, levels) = rest[: len(spans)], rest[len(spans) :]
    send_out(own_ref, low, part, with_scales(refs, spans, own_ref.shape[1]), out_ref, levels)


def combine(own, low, part, arrived, after):
    _, rows, slices = own.shape
    return pl.pallas_call(
        functools.partial(combine_kernel, low, part, [(0, part)] * len(arrived)),
        in_specs=[VMEM, ANY] + [VMEM] * len(arrived),
        out_specs=VMEM,
        out_shape=payload_of(part, rows, slices),
        scratch_shapes=[pltpu.VMEM((round_up(part, 16), slices), jnp.float32)],
        compiler_params=PARAMS,
        cost_estimate=QUICK,
    )(own, after, *arrived)


def gather_kernel(spans, own_ref, *rest):
    refs, out_ref = rest[: len(spans)], rest[len(spans)]
    arrived = with_scales(refs, spans, own_ref.shape[1])
    for t in range(out_ref.shape[0]):
        out_ref[t] = joined(own_ref[t], t, arrived)


def gather(own, tiles, spans, arrived):
    return pl.pallas_call(
        functools.partial(gather_kernel, spans),
        in_specs=[VMEM] * (1 + len(arrived)),
        out_specs=VMEM,
        out_shape=jax.ShapeDtypeStruct((tiles,) + own.shape[1:], jnp.float32),
        compiler_params=PARAMS,
        cost_estimate=QUICK,
    )(own, *arrived)


def weight_kernel(table_ref, index_ref, after, out_ref):
    looked = jnp.zeros(index_ref.shape, jnp.float32)
    for c in range(table_ref.shape[0]):
        looked = jnp.where(index_ref[...] == c, table_ref[c], looked)
    for t in range(index_ref.shape[0]):
        wide = jnp.broadcast_to(looked[t : t + 1, :], (out_ref.shape[2], out_ref.shape[1]))
        out_ref[t] = wide.T.astype(jnp.bfloat16)


def ray_weights(table, index, slices, after):
    tiles, rows = index.shape
    return pl.pallas_call(
        weight_kernel,
        in_specs=[SMEM, VMEM, ANY],
        out_specs=VMEM,
        out_shape=jax.ShapeDtypeStruct((tiles, rows, slices), jnp.bfloat16),
        compiler_params=PARAMS,
        cost_estimate=QUICK,
    )(table.astype(jnp.float32), index, after)


def residual_kernel(spans, sum_ref, sinogram_ref, weight_ref, *rest):
    refs, out_refs = rest[: len(spans)], rest[len(spans) :]
    arrived = with_scales(refs, spans, sum_ref.shape[1])
    part = out_refs[0].shape[0]
    for t in range(sum_ref.shape[0]):
        gap = sinogram_ref[t].astype(jnp.float32) - joined(sum_ref[t], t, arrived)
        out_refs[t // part][t % part] = (weight_ref[t].astype(jnp.float32) * gap).astype(
            jnp.bfloat16
        )


def residual_of(sums, sinogram, weights, part, spans, arrived):
    tiles, rows, slices = sinogram.shape
    return pl.pallas_call(
        functools.partial(residual_kernel, spans),
        in_specs=[VMEM] * (3 + len(arrived)),
        out_specs=[VMEM] * (tiles // part),
        out_shape=[jax.ShapeDtypeStruct((part, rows, slices), jnp.bfloat16)] * (tiles // part),
        compiler_params=PARAMS,
        cost_estimate=QUICK,
    )(sums, sinogram, weights, *arrived)


def column_kernel(table_ref, projector_ref, after, out_ref):
    slots, per_slot, rows, cols = projector_ref.shape
    out_ref[...] = jnp.zeros_like(out_ref)

    @pl.loop(0, slots)
    def _(s):
        for g in range(per_slot):
            column = jnp.sum(projector_ref[s, g].astype(jnp.float32), axis=0, keepdims=True)
            out_ref[table_ref[8 + g, s]] += column


def column_sums(table, projector, patch_tiles, after):
    slots, per_slot, rows, cols = projector.shape
    return pl.pallas_call(
        column_kernel,
        in_specs=[SMEM, VMEM, ANY],
        out_specs=VMEM,
        out_shape=jax.ShapeDtypeStruct((patch_tiles, 1, cols), jnp.float32),
        compiler_params=PARAMS,
        cost_estimate=QUICK,
    )(table, projector, after)


def spread_kernel(lows, begin, finish, table_from, projector_ref, *rest):
    rest = list(rest)
    before = None if begin else rest.pop(0)
    volume_ref, column_ref = (rest.pop(0), rest.pop(0)) if finish else (None, None)
    chunks, (out_ref, table_ref, sem, slot_list, held) = rest[: len(lows)], rest[len(lows) : len(lows) + 5]
    total = rest[-1]
    copy = pltpu.make_async_copy(table_from, table_ref, sem)
    copy.start()
    slots, per_slot, rows, cols = projector_ref.shape
    part = chunks[0].shape[0]
    patch_tiles = total.shape[0] - 1
    for low, chunk in zip(lows, chunks):
        held[low : low + part] = chunk[...]
    if begin:
        total[...] = jnp.zeros_like(total)
    else:
        total[...] = before[...]
    copy.wait()
    count = list_slots(table_ref.at[0], (0, slots), [(low, low + part) for low in lows], slot_list)

    @pl.loop(0, (count + UNROLL - 1) // UNROLL)
    def _(i):
        parts, places = [], []
        for u in range(UNROLL):
            real = i * UNROLL + u < count
            s = jnp.where(real, slot_list[i * UNROLL + u], slot_list[0])
            right = jnp.concatenate([projector_ref[s, g] for g in range(per_slot)], axis=1)
            parts.append(
                lax.dot_general(
                    held[table_ref[0, s]], right, (((0,), (0,)), ((), ())), preferred_element_type=jnp.float32
                )
            )
            places.append([jnp.where(real, table_ref[8 + g, s], patch_tiles) for g in range(per_slot)])
        for part, place in zip(parts, places):
            for g in range(per_slot):
                total[place[g]] += part[:, g * cols : (g + 1) * cols]

    if finish:
        stage, sems = rest[len(lows) + 5 : len(lows) + 7]
        copies = []
        for q in range(patch_tiles):
            stage[q] = volume_ref[q].astype(jnp.float32) + (total[q] / column_ref[q]).T
            copies.append(pltpu.make_async_copy(stage.at[q], out_ref.at[q], sems.at[q]))
            copies[-1].start()
        for copy in copies:
            copy.wait()


def spread(table, projector, all_cells, lows, chunks, patch_tiles, before, last=()):
    slots, per_slot, rows, cols = projector.shape
    slices = chunks[0].shape[2]
    begin, finish = before is None, bool(last)
    more = ([] if begin else [before]) + list(last) + chunks
    shape = (patch_tiles + 1, slices, cols)
    scratch = [
        pltpu.SMEM(table.shape, jnp.int32),
        pltpu.SemaphoreType.DMA,
        pltpu.SMEM((slots + UNROLL,), jnp.int32),
        pltpu.VMEM((all_cells, rows, slices), jnp.bfloat16),
    ]
    kernel = functools.partial(spread_kernel, lows, begin, finish)
    if not finish:
        inner = kernel
        kernel = lambda *refs: inner(*refs, refs[-5])
    return pl.pallas_call(
        kernel,
        in_specs=[VMEM] * (2 + len(more)),
        out_specs=HBM if finish else VMEM,
        out_shape=jax.ShapeDtypeStruct((patch_tiles, cols, slices) if finish else shape, jnp.float32),
        scratch_shapes=scratch
        + (
            [
                pltpu.VMEM((patch_tiles, cols, slices), jnp.float32),
                pltpu.SemaphoreType.DMA((patch_tiles,)),
                pltpu.VMEM(shape, jnp.float32),
            ]
            if finish
            else []
        ),
        compiler_params=PARAMS,
        cost_estimate=QUICK,
    )(table, projector, *more)


def gate(value, *after, weight=0):
    return pl.pallas_call(
        lambda *refs: None,
        in_specs=[VMEM] * (1 + len(after)),
        out_specs=VMEM,
        out_shape=jax.ShapeDtypeStruct(value.shape, value.dtype),
        input_output_aliases={0: 0},
        compiler_params=PARAMS,
        cost_estimate=weighs(weight),
    )(value, *after)


def dense_plan(volume, projector, slot_ray, slot_pixel, sinogram, weight_index, weight_table):
    inners = lax.axis_size("inner")
    outers = lax.axis_size("outer")
    tiles = sinogram.shape[0]
    patch_tiles, _, slices = volume.shape
    sizes = (outers, inners, tiles)
    pixel = slot_pixel.T

    turns = sorted(range(inners), key=lambda k: (bin(k).count("1"), k))
    far = [k for k in reversed(turns) if k > 1]
    others = range(1, outers)
    low = lambda j, k: (j * inners + k) * tiles
    arrived = {(j, k): [] for j in range(outers) for k in range(inners)}
    first, *sent = [(j, k) for k in far[:1] for j in others]
    near = [(j, 1) for j in others]
    sent += [(j, k) for k in far[1:] for j in others]
    payload, projector, volume, table = first_send(
        slot_ray, pixel, projector, volume, sizes, low(*first)
    )
    kept = [(0, inners * tiles)] + [(low(j, 0), low(j, 0) + tiles) for j in others]
    sends = {first: payload}
    payloads = further_sums(
        table, projector, volume, tiles, [low(*piece) for piece in near], [], payload
    )
    sends.update(zip(near, payloads))
    kept = [(low(0, 2), low(1, 0)), (0, low(0, 2)), (low(1, 0), low(1, 0) + tiles)]
    *payloads, own = further_sums(
        table, projector, volume, tiles, [low(*piece) for piece in sent], kept[:1], payloads[-1]
    )
    sends.update(zip(sent, payloads))
    for k in far[:1]:
        for j in others:
            arrived[0, k].append(gate(swap(sends[j, k], "outer", j), weight=4))
    for j in others:
        arrived[j, 0].append(swap(sends[j, 1], "inner", 1))
    after = own
    for i, k in enumerate(far):
        bit = k & -k
        after = combine(own, low(0, k) - low(0, 2), tiles, arrived[0, k], after)
        arrived[0, k ^ bit].append(swap(after, "inner", bit) if i == 0 else gate(swap(after, "inner", bit)))
        if i == 0:
            (near_own,) = further_sums(table, projector, volume, tiles, [], kept[1:], after)
            for l in far[1:]:
                for j in others:
                    payload = gate(sends[j, l], after) if LATER else sends[j, l]
                    arrived[0, l].append(swap(payload, "outer", j))
            for j in others:
                after = combine(near_own, 2 * tiles, tiles, arrived[j, 0], after)
                arrived[0, 0].append(swap(after, "outer", j))
    after = combine(near_own, tiles, tiles, [], after)
    arrived[0, 0].append(gate(swap(after, "inner", 1)))
    columns = column_sums(table, projector, patch_tiles, after)
    weights = ray_weights(weight_table, weight_index, slices, columns)
    longest = arrived[0, 0][-2:]
    rest = arrived[0, 0][:-2]
    span = (0, tiles)
    sums = gather(near_own, tiles, [span] * len(longest), longest)
    residual = residual_of(sums, sinogram, weights, tiles, [span] * len(rest), rest)[0]

    chunks = {(0, 0): residual}
    total = None

    def add(pieces, last=()):
        nonlocal total
        total = spread(
            table, projector, outers * inners * tiles, [low(*piece) for piece in pieces],
            [chunks[piece] for piece in pieces], patch_tiles, total, last,
        )

    chunks[0, 2] = swap(residual, "inner", 2)
    chunks[0, 1] = gate(swap(residual, "inner", 1), weight=2)
    chunks[1, 0] = swap(residual, "outer", 1)
    chunks[0, 3] = swap(chunks[0, 2], "inner", 1)
    chunks[1, 2] = swap(chunks[0, 2], "outer", 1)
    done = [(0, 0), (0, 1), (0, 2), (1, 0)]
    add(done)
    chunks[0, 3] = gate(chunks[0, 3], total)
    chunks[1, 3] = swap(chunks[0, 3], "outer", 1)
    chunks[1, 1] = swap(gate(chunks[1, 0], chunks[0, 3]), "inner", 1)
    add([(0, 3), (1, 2)])
    add([(1, 3), (1, 1)], (volume, columns))
    return total


def slot_plan(volume, projector, slot_ray, slot_pixel, sinogram, weight_index, weight_table):
    inners = lax.axis_size("inner")
    outers = lax.axis_size("outer")
    slot_count = projector.shape[0]
    per_slot = projector.shape[1]
    tile_rows = projector.shape[2]
    tile_cols = projector.shape[3]
    patch_tiles = volume.shape[0]
    slice_count = volume.shape[2]
    owned_rows = sinogram.shape[0]
    band_rows = owned_rows * outers
    capacity = 2 * slot_count // inners
    cell_count = inners * capacity
    target = slot_ray // band_rows
    offset = slot_ray % band_rows
    same_target = target[:, None] == target[None, :]
    earlier = jnp.arange(slot_count)[:, None] > jnp.arange(slot_count)[None, :]
    slot_rank = jnp.sum(jnp.logical_and(same_target, earlier), axis=1)
    position = target * capacity + slot_rank
    partial_value = jnp.zeros((slot_count, tile_rows, slice_count), jnp.float32)
    for column in range(per_slot):
        pixels = volume[slot_pixel[:, column]]
        partial_value = partial_value + jnp.einsum(
            "srp,spc->src", projector[:, column], pixels, preferred_element_type=jnp.float32
        )
    outgoing = (
        jnp.zeros((cell_count, tile_rows, slice_count), jnp.float32).at[position].set(partial_value)
    )
    labels = jnp.full((cell_count,), -1.0, jnp.float32).at[position].set(offset.astype(jnp.float32))
    arrived, arrived_rows = (
        lax.all_to_all(
            outgoing.reshape(inners, capacity, tile_rows, slice_count),
            "inner",
            split_axis=0,
            concat_axis=0,
            tiled=True,
        ),
        lax.all_to_all(
            labels.reshape(inners, capacity), "inner", split_axis=0, concat_axis=0, tiled=True
        ),
    )
    selector = (
        jnp.arange(band_rows, dtype=jnp.float32)[:, None] == arrived_rows.reshape(1, cell_count)
    ).astype(jnp.float32)
    block_sums = jnp.dot(
        selector,
        arrived.reshape(cell_count, tile_rows * slice_count),
        precision=lax.Precision.HIGHEST,
    ).reshape(band_rows, tile_rows, slice_count)
    classes = weight_table.shape[0]
    lookup = weight_index[:, :, None] == jnp.arange(classes)[None, None, :]
    weights = jnp.sum(
        jnp.where(lookup, weight_table[None, None, :], jnp.zeros((), weight_table.dtype)), axis=2
    )
    own_sums = lax.psum_scatter(block_sums, "outer", scatter_dimension=0, tiled=True)
    own_residual = (
        weights.astype(jnp.float32)[:, :, None] * (sinogram.astype(jnp.float32) - own_sums)
    ).astype(jnp.bfloat16)
    residual = lax.all_gather(own_residual, "outer", axis=0, tiled=True)
    picked = jnp.dot(
        selector.T.astype(jnp.bfloat16),
        residual.reshape(band_rows, tile_rows * slice_count),
        preferred_element_type=jnp.float32,
    ).astype(jnp.bfloat16)
    returned = lax.all_to_all(
        picked.reshape(inners, capacity, tile_rows, slice_count),
        "inner",
        split_axis=0,
        concat_axis=0,
        tiled=True,
    )
    slot_residual = returned.reshape(cell_count, tile_rows, slice_count)[position]
    owners = jnp.arange(patch_tiles)
    backward_sum = jnp.zeros((patch_tiles, tile_cols, slice_count), jnp.float32)
    column_sum = jnp.zeros((patch_tiles, tile_cols), jnp.float32)
    for column in range(per_slot):
        member = (owners[:, None] == slot_pixel[None, :, column]).astype(jnp.float32)
        spread = jnp.einsum(
            "srp,src->spc", projector[:, column], slot_residual, preferred_element_type=jnp.float32
        )
        backward_sum = backward_sum + jnp.einsum(
            "ts,spc->tpc", member, spread, precision=lax.Precision.HIGHEST
        )
        column_sum = column_sum + jnp.dot(
            member,
            jnp.sum(projector[:, column], axis=1, dtype=jnp.float32),
            precision=lax.Precision.HIGHEST,
        )
    return volume.astype(jnp.float32) + backward_sum / column_sum[:, :, None]


def on_device(volume, projector, slot_ray, slot_pixel, sinogram, weight_index, weight_table):
    inners = lax.axis_size("inner")
    outers = lax.axis_size("outer")
    capacity = 2 * slot_ray.shape[0] // inners
    dense = (inners, outers) == (4, 2) and sinogram.shape[0] * outers <= capacity
    plan = dense_plan if dense else slot_plan
    return plan(volume, projector, slot_ray, slot_pixel, sinogram, weight_index, weight_table)


def solution(mesh):
    in_specs = (
        P(("group", "inner", "outer"), None, "cuts"),
        P(("inner", "outer"), None, None, None),
        P(("inner", "outer")),
        P(("inner", "outer"), None),
        P(("group", "inner", "outer"), None, "cuts"),
        P(("group", "inner", "outer"), None),
        P(),
    )
    out_specs = P(("group", "inner", "outer"), None, "cuts")
    return jax.shard_map(
        on_device, mesh=mesh, in_specs=in_specs, out_specs=out_specs, check_vma=False
    )
```
